32 devices in a mesh: flop: 4 (over z), turn: 4 (over y, core), river: 2 (over x).
Axes of the slice: x: 2, y: 2, z: 4, core: 2. Of those that a mesh axis runs over, the one named last changes fastest.
Arguments:
- regrets: float32 [4, 256, 1326], P('flop', ('turn', 'river')), may hold values from -6 to 6
- opp_reach: bfloat16 [4, 256, 1326], P('flop', ('turn', 'river')), may hold values from 0 to 1
- pot_size: int32 [4, 256], P('flop', ('turn', 'river')), may hold values from 1 to 8
- line_kind: int32 [4, 256], P('flop', ('turn', 'river')), may hold values from 0 to 2
- board_lines: int32 [4, 4, 4, 256], P('flop', 'turn', 'river'), may hold values from 0 to 255, as said below
- board_count: int32 [4, 4, 4], P('flop', 'turn', 'river'), may hold values from 64 to 256, as said below
- hand_ranks: int32 [4, 4, 4, 1326], P('flop', 'turn', 'river'), may hold values from 0 to 7461
- live_hands: int32 [4, 4, 4, 1326], P('flop', 'turn', 'river'), may hold values 0 or 1
Outputs:
- new_regrets: float32 [4, 256, 1326], P('flop', ('turn', 'river'))
- chance_values: float32 [128, 1326], P(('turn', 'river'))
The draws below stay inside these ranges and needn't reach their ends.
Inputs may be any that keep to these rules, and one draw needn't show every extreme that they name: `board_lines`: each board lists 256 different lines of its flop; its first board_count slots hold the lines live on it, the other slots add nothing. `board_count`: in every flop one board has all 256 slots live and another only 64.
All inputs are finite; a program needn't handle non-finite values. No bound on the sum of `live_hands` on one device may be relied on, other than what follows from the above.
Results may differ from the reference program's by a relative error of at most 0.0003.
Values may be sent and summed in bfloat16 or wider, within the bound.
No kernel may reach another device: no remote copies, remote signals or barrier semaphores. Data moves between devices by JAX's collectives and lax.ppermute only.
A program may use at most 64 MiB of HBM per device.

```python
import jax
import jax.numpy as jnp
import numpy as np
from jax import lax

CARDS = 52
H = 1326
ACTS = 2
LINES = 256
CAP = 256
FLOPS = 4
TURNS = 4
RIVERS = 4
N_FLOP = 4


def draw_board_lines(key, part):
    board_total = FLOPS * TURNS * RIVERS
    line_keys = jax.random.split(jax.random.fold_in(key, 11), board_total)
    orders = jax.vmap(lambda board_key: jax.random.permutation(board_key, LINES)[:CAP])(line_keys)
    return orders.reshape(FLOPS, TURNS, RIVERS, CAP).astype(jnp.int32)


def draw_board_count(key, part):
    board_total = TURNS * RIVERS
    live_counts = jax.random.randint(jax.random.fold_in(key, 23), (FLOPS, board_total), CAP // 4, CAP + 1)
    full_board = jax.random.randint(jax.random.fold_in(key, 29), (FLOPS, 1), 0, board_total)
    light_step = jax.random.randint(jax.random.fold_in(key, 31), (FLOPS, 1), 1, max(board_total, 2))
    light_board = (full_board + light_step) % board_total
    board_index = jnp.arange(board_total, dtype=jnp.int32)[None, :]
    live_counts = jnp.where(board_index == light_board, CAP // 4, live_counts)
    live_counts = jnp.where(board_index == full_board, CAP, live_counts)
    return live_counts.reshape(FLOPS, TURNS, RIVERS).astype(jnp.int32)


def place_ends(entries, rng, low, top_value):
    longest = entries.shape.index(max(entries.shape))
    spots = []
    for shift in (0, 1):
        where = [jax.random.randint(jax.random.fold_in(rng, axis), (), 0, length) for axis, length in enumerate(entries.shape)]
        where[longest] = (where[longest] + shift) % entries.shape[longest]
        spots.append(tuple(where))
    return entries.at[spots[0]].set(low).at[spots[1]].set(top_value)


def block_scale(own_key, dims, pieces, least, top_value):
    gain, own = 1.0, jax.random.fold_in(own_key, 6)
    for position, blocks in pieces:
        heights = jnp.exp(jax.random.uniform(jax.random.fold_in(own, position), (blocks,), jnp.float32, least / len(pieces), top_value / len(pieces)))
        gain = gain * jnp.repeat(heights, dims[position] // blocks).reshape([-1 if axis == position else 1 for axis in range(len(dims))])
    return gain


def gaussian(stream_key, shape, width, limit, pieces=(), held_as=jnp.bfloat16):
    level = block_scale(stream_key, shape, pieces, -0.22, 0.18) if pieces else 1.0
    array = jax.random.normal(stream_key, shape, jnp.float32) * width * level
    return jnp.minimum(jnp.maximum(array, -limit), limit).astype(held_as)


def setup_inputs(seed: int = 0) -> dict:
    keys = jax.random.split(jax.random.key(seed), 9)
    return {
        "regrets": gaussian(keys[0], (FLOPS, LINES, H), 1.0, 6.0, ((0, 4), (1, 8)), jnp.float32),
        "opp_reach": jnp.clip(1.0 * jax.random.uniform(keys[1], (FLOPS, LINES, H), jnp.float32) ** block_scale(keys[1], (FLOPS, LINES, H), ((0, 4), (1, 8)), -0.2, 0.2), 0.0, 1.0).astype(jnp.bfloat16),
        "pot_size": place_ends(jax.random.randint(keys[2], (FLOPS, LINES), 1, 9), jax.random.fold_in(keys[2], 1), 1, 8).astype(jnp.int32),
        "line_kind": place_ends(jax.random.randint(keys[3], (FLOPS, LINES), 0, 3), jax.random.fold_in(keys[3], 1), 0, 2).astype(jnp.int32),
        "board_lines": draw_board_lines(jax.random.fold_in(keys[8], 71), 0),
        "board_count": draw_board_count(jax.random.fold_in(keys[8], 71), 0),
        "hand_ranks": place_ends(jax.random.randint(keys[6], (FLOPS, TURNS, RIVERS, H), 0, 7462), jax.random.fold_in(keys[6], 1), 0, 7461).astype(jnp.int32),
        "live_hands": place_ends((jax.random.randint(keys[7], (FLOPS, TURNS, RIVERS, H), 0, 1000) < 815).astype(jnp.int32), jax.random.fold_in(keys[7], 1), 0, 1),
    }


floor_share = 0.1


def disjoint_table(card_count):
    card_first, card_second = np.triu_indices(card_count, 1)
    first_cards = jnp.asarray(card_first.astype(np.int32))
    second_cards = jnp.asarray(card_second.astype(np.int32))
    apart = (first_cards[:, None] != first_cards[None, :]) & (first_cards[:, None] != second_cards[None, :])
    apart = apart & (second_cards[:, None] != first_cards[None, :]) & (second_cards[:, None] != second_cards[None, :])
    return apart


def payoff_matrix(board_ranks, board_live, apart):
    both_live = apart & (board_live[:, None] > 0) & (board_live[None, :] > 0)
    fold_part = both_live.astype(jnp.float32)
    ordering = jnp.sign(board_ranks[None, :] - board_ranks[:, None]).astype(jnp.float32)
    return jnp.concatenate([fold_part * ordering, fold_part], axis=1)


def reference(regrets, opp_reach, pot_size, line_kind, board_lines, board_count, hand_ranks, live_hands):
    hand_count = opp_reach.shape[2]
    apart = disjoint_table(CARDS)
    chance_scale = 1.0 / (TURNS * RIVERS * hand_count)
    pot_float = pot_size.astype(jnp.float32)
    show_coef = jnp.where(line_kind == 0, pot_float, 0.0)
    fold_coef = jnp.where(line_kind == 1, -pot_float, jnp.where(line_kind == 2, pot_float, 0.0))
    slot_index = jnp.arange(CAP, dtype=jnp.int32)
    flop_values = []
    for flop_index in range(N_FLOP):
        reach_rows = opp_reach[flop_index].astype(jnp.float32)
        line_coef = jnp.stack([show_coef[flop_index], fold_coef[flop_index]], axis=1)

        def add_board(running, board_item):
            slot_lines, live_count, board_ranks, board_live = board_item
            matrix = payoff_matrix(board_ranks, board_live, apart)
            slot_reach = jnp.take(reach_rows, slot_lines, axis=0)
            products = jnp.dot(slot_reach, matrix, precision=lax.Precision.HIGHEST)
            slot_coef = jnp.take(line_coef, slot_lines, axis=0)
            keep_mask = (slot_index < live_count).astype(jnp.float32)
            board_value = (slot_coef[:, 0:1] * products[:, :hand_count] + slot_coef[:, 1:2] * products[:, hand_count:]) * (chance_scale * keep_mask)[:, None]
            return running.at[slot_lines].add(board_value), None

        items = (board_lines[flop_index].reshape(-1, CAP), board_count[flop_index].reshape(-1),
                 hand_ranks[flop_index].reshape(-1, hand_count), live_hands[flop_index].reshape(-1, hand_count))
        summed, _ = lax.scan(add_board, jnp.zeros((LINES, hand_count), jnp.float32), items)
        flop_values.append(summed)
    line_values = jnp.stack(flop_values)
    grouped = regrets.reshape(N_FLOP, LINES // ACTS, ACTS, hand_count)
    worth_lines = line_values.reshape(N_FLOP, LINES // ACTS, ACTS, hand_count)
    positive = jnp.maximum(grouped, 0.0)
    strategy = (positive + floor_share) / (jnp.sum(positive, axis=2, keepdims=True) + ACTS * floor_share)
    node_values = jnp.sum(strategy * worth_lines, axis=2)
    new_regrets = jnp.maximum(grouped + worth_lines - node_values[:, :, None, :], 0.0).reshape(regrets.shape)
    chance_values = jnp.sum(node_values, axis=0) / N_FLOP
    return (new_regrets, chance_values)
```

```python
import functools

import jax
import jax.numpy as jnp
import numpy as np
from jax import lax
from jax.experimental import pallas as pl
from jax.experimental.pallas import tpu as pltpu
from jax.sharding import PartitionSpec as P

CARDS = 52
ACTS = 2
LANE = 128
SUB = 16
RANK_SPAN = 8192
ROW_TILE = 128
COL_TILE = 512

floor_share = 0.1


def up(value, unit):
    return -(-value // unit) * unit


def tiles(total, size):
    return [(first, min(size, total - first)) for first in range(0, total, size)]


@functools.cache
def tables(hand_count):
    wide, deep = up(hand_count, LANE), up(hand_count, SUB)
    first, second = np.triu_indices(CARDS, 1)
    cards = np.zeros((hand_count, CARDS), np.float32)
    cards[np.arange(hand_count), first] = 1
    cards[np.arange(hand_count), second] = 1
    apart = np.zeros((deep, wide), np.float32)
    apart[:hand_count, :hand_count] = (cards @ cards.T) == 0
    sums = np.concatenate([np.ones((hand_count, 1), np.float32), cards], axis=1)
    parts = sums.shape[1]
    collect = np.zeros((wide, LANE), np.float32)
    spread = np.zeros((LANE, wide), np.float32)
    signed = sums.copy()
    signed[:, 1:] *= -1
    for copy in range(2):
        collect[:hand_count, copy * parts : (copy + 1) * parts] = sums
        spread[copy * parts : (copy + 1) * parts, :hand_count] = signed.T
    dtype = jnp.bfloat16
    return apart.astype(dtype), (-apart).astype(dtype), collect.astype(dtype), spread.astype(dtype)


def boards_kernel(hand_count, line_count, base_ref, own_ref, mate_ref, *refs, boards_in):
    board_refs, refs = refs[:boards_in], refs[boards_in:]
    apart_ref, minus_ref, collect_ref, spread_ref, own_out, mate_out, column_ref, board_ref = refs
    wide = up(hand_count, LANE)
    deep = apart_ref.shape[0]
    rows = own_ref.shape[0]
    parts = 1 + CARDS
    reach = jnp.concatenate([own_ref[...], mate_ref[...]], axis=0)
    kind = reach[:, hand_count : hand_count + 1].astype(jnp.float32)
    row = lax.broadcasted_iota(jnp.int32, (2 * rows, 1), 0)
    within = jnp.where(row < rows, row, row - rows)
    line = jnp.where(row < rows, base_ref[0], base_ref[1]) + within
    line = jnp.where(within < line_count, line, -2)
    lane = lax.broadcasted_iota(jnp.int32, (2 * rows, LANE), 1)
    own_out[...] = jnp.zeros_like(own_out)
    mate_out[...] = jnp.zeros_like(mate_out)

    first = 0
    for ref in board_refs:
        board_ref[first : first + ref.shape[0]] = ref[...]
        first += ref.shape[0]

    @pl.loop(0, first)
    def add_board(board):
        keys = board_ref[pl.ds(board, 1), :wide]
        slots = board_ref[pl.ds(board, 1), wide:]
        ranks = (keys & (RANK_SPAN - 1)).astype(jnp.float32)
        live = (keys >> (RANK_SPAN.bit_length() - 1)).astype(jnp.float32)
        keep = jnp.max(jnp.where(slots == line, 1.0, 0.0), axis=1, keepdims=True)
        show_keep = jnp.where(kind == 0, keep, 0.0).astype(jnp.bfloat16)
        fold_keep = jnp.where(kind == 0, 0.0, keep).astype(jnp.bfloat16)
        held = reach * live.astype(jnp.bfloat16)
        show_reach = held * show_keep
        fold_reach = held * fold_keep
        sums = jnp.dot(fold_reach, collect_ref[...], preferred_element_type=jnp.float32)
        high = sums.astype(jnp.bfloat16)
        low = (sums - high.astype(jnp.float32)).astype(jnp.bfloat16)
        sums = jnp.where(lane < parts, high.astype(jnp.float32), low.astype(jnp.float32)).astype(jnp.bfloat16)
        column_ref[...] = jnp.transpose(jnp.broadcast_to(ranks, (LANE, wide)))[:deep]
        for first, count in tiles(wide, COL_TILE):
            at = slice(first, first + count)
            total = jnp.dot(sums, spread_ref[:, at], preferred_element_type=jnp.float32)
            for top, height in tiles(deep, ROW_TILE):
                down = slice(top, top + height)
                column = jnp.concatenate([column_ref[down]] * (count // LANE), axis=1)
                order = (ranks[:, at] - column).astype(jnp.bfloat16)
                matrix = jnp.minimum(jnp.maximum(order, minus_ref[down, at]), apart_ref[down, at])
                total += jnp.dot(show_reach[:, down], matrix, preferred_element_type=jnp.float32)
            total = (total + fold_reach[:, at].astype(jnp.float32)) * live[:, at]
            own_out[:, at] += total[:rows]
            mate_out[:, at] += total[rows:]


def board_sums(hand_count, line_count, base, own, mate, boards):
    rows, wide = own.shape
    consts = [jnp.asarray(table) for table in tables(hand_count)]
    whole = pl.BlockSpec(memory_space=pltpu.VMEM)
    out = jax.ShapeDtypeStruct((rows, wide), jnp.float32)
    return pl.pallas_call(
        functools.partial(boards_kernel, hand_count, line_count, boards_in=len(boards)),
        out_shape=(out, out),
        in_specs=[pl.BlockSpec(memory_space=pltpu.SMEM)] + [whole] * (2 + len(boards) + len(consts)),
        out_specs=(whole, whole),
        scratch_shapes=[
            pltpu.VMEM((consts[0].shape[0], LANE), jnp.float32),
            pltpu.VMEM((sum(board.shape[0] for board in boards), boards[0].shape[1]), jnp.int32),
        ],
        compiler_params=pltpu.CompilerParams(vmem_limit_bytes=40 << 20),
        name="board_sums",
    )(base, own, mate, *boards, *consts)


def update_kernel(hand_count, scale, own_ref, mate_ref, reach_ref, regret_ref, regret_out, node_out, node_ref):
    coef = reach_ref[:, hand_count + 1 : hand_count + 2].astype(jnp.float32) * scale
    values = (own_ref[:, :hand_count] + mate_ref[:, :hand_count]) * coef
    regrets = regret_ref[...]
    rows = regrets.shape[0]
    even = lax.broadcasted_iota(jnp.int32, (rows, 1), 0) % ACTS == 0

    def both(array):
        other = jnp.where(even, pltpu.roll(array, rows - 1, 0), pltpu.roll(array, 1, 0))
        return array + other

    positive = jnp.maximum(regrets, 0.0)
    strategy = (positive + floor_share) / (both(positive) + ACTS * floor_share)
    node = both(strategy * values)
    regret_out[...] = jnp.maximum(regrets + values - node, 0.0)
    for tile, (first, count) in enumerate(tiles(hand_count, LANE)):
        node_ref[tile, :, :count] = node[:, first : first + count]
        picked = node_ref[tile, pl.ds(0, rows // ACTS, stride=ACTS), :]
        node_out[:, first : first + count] = picked[:, :count]


def update(hand_count, scale, own, mate, reach, regrets):
    rows = regrets.shape[0]
    whole = pl.BlockSpec(memory_space=pltpu.VMEM)
    return pl.pallas_call(
        functools.partial(update_kernel, hand_count, scale),
        out_shape=(
            jax.ShapeDtypeStruct((rows, hand_count), jnp.float32),
            jax.ShapeDtypeStruct((rows // ACTS, hand_count), jnp.float32),
        ),
        in_specs=[whole] * 4,
        out_specs=(whole, whole),
        scratch_shapes=[pltpu.VMEM((-(-hand_count // LANE), rows, LANE), jnp.float32)],
        name="regret_update",
    )(own, mate, reach, regrets)


def swap(array, axes, mask):
    return lax.ppermute(array, axes, [(index, index ^ mask) for index in range(lax.axis_size(axes))])


def on_device(
    regrets, opp_reach, pot_size, line_kind, board_lines, board_count, hand_ranks, live_hands
):
    hand_count = opp_reach.shape[2]
    line_count = opp_reach.shape[1]
    group = ("turn", "river")
    group_size = lax.axis_size(group)
    core = lax.axis_size("river")
    board_total = group_size * board_lines.shape[2]
    rows, wide = up(line_count, SUB), up(hand_count, LANE)

    keys = hand_ranks[0, 0] + RANK_SPAN * live_hands[0, 0]
    slot = lax.broadcasted_iota(jnp.int32, board_lines.shape[2:], 1)
    slots = jnp.where(slot < board_count[0, 0][:, None], board_lines[0, 0], -1)
    boards = jnp.concatenate([jnp.pad(keys, ((0, 0), (0, wide - hand_count))), slots], axis=1)
    coef = jnp.where(line_kind == 1, -pot_size, pot_size)
    terms = jnp.concatenate([line_kind, coef], axis=0).astype(jnp.bfloat16).T
    reach = jnp.concatenate([opp_reach[0], terms], axis=1)
    reach = jnp.pad(reach, ((0, rows - line_count), (0, wide - reach.shape[1])))

    mate_reach = swap(reach, group, core)
    masks = [mask for mask in range(1, group_size) if not mask & core]
    if len(masks) < 4:
        boards = [boards] + [swap(boards, group, mask) for mask in masks]
    else:
        for mask in masks:
            if mask & (mask - 1) == 0:
                boards = jnp.concatenate([boards, swap(boards, group, mask)], axis=0)
        boards = [boards]
    index = lax.axis_index(group)
    base = jnp.stack([index, index ^ core]).astype(jnp.int32) * line_count
    own, for_mate = board_sums(hand_count, line_count, base, reach, mate_reach, boards)
    mate = swap(for_mate, group, core)
    held = jnp.pad(regrets[0], ((0, rows - line_count), (0, 0)))
    updated, node = update(hand_count, 1.0 / (board_total * hand_count), own, mate, reach, held)
    updated, node = updated[:line_count], node[: line_count // ACTS]
    flops = lax.axis_size("flop")
    total = node + swap(node, "flop", 1)
    for mask in range(2, flops, 2):
        total += swap(node, "flop", mask) + swap(node, "flop", mask + 1)
    return (updated[None], total / flops)


def solution(mesh):
    placed = (
        P("flop", ("turn", "river"), None),
        P("flop", ("turn", "river"), None),
        P("flop", ("turn", "river")),
        P("flop", ("turn", "river")),
        P("flop", "turn", "river", None),
        P("flop", "turn", "river"),
        P("flop", "turn", "river", None),
        P("flop", "turn", "river", None),
    )
    return jax.shard_map(
        on_device,
        mesh=mesh,
        in_specs=placed,
        out_specs=(P("flop", ("turn", "river"), None), P(("turn", "river"), None)),
        check_vma=False,
    )
```

```python
import functools

import jax
import jax.numpy as jnp
import numpy as np
from jax import lax
from jax.experimental import pallas as pl
from jax.experimental.pallas import tpu as pltpu
from jax.sharding import PartitionSpec as P

CARDS = 52
ACTS = 2
LANE = 128
SUB = 32
RANK_SPAN = 8192
MANTISSA = 128
ROW_TILE = 128
COL_TILE = 768
UNROLL = 8
STEPS = 32767.0
LOWEST = 100
WHOLE = pl.BlockSpec(memory_space=pltpu.VMEM)
SCALARS = pl.BlockSpec(memory_space=pltpu.SMEM)

floor_share = 0.1


def up(value, unit):
    return -(-value // unit) * unit


def tiles(total, size):
    return [(first, min(size, total - first)) for first in range(0, total, size)]


def params(mebibytes):
    return pltpu.CompilerParams(vmem_limit_bytes=mebibytes << 20)


@functools.cache
def tables(hand_count):
    wide, deep = up(hand_count, LANE), up(hand_count, 16)
    first, second = np.triu_indices(CARDS, 1)
    cards = np.zeros((hand_count, CARDS), np.float32)
    cards[np.arange(hand_count), first] = 1
    cards[np.arange(hand_count), second] = 1
    apart = np.zeros((deep, wide), np.float32)
    apart[:hand_count, :hand_count] = (cards @ cards.T) == 0
    sums = np.concatenate([np.ones((hand_count, 1), np.float32), cards], axis=1)
    parts = sums.shape[1]
    collect = np.zeros((wide, LANE), np.float32)
    spread = np.zeros((LANE, wide), np.float32)
    signed = sums.copy()
    signed[:, 1:] *= -1
    for copy in range(2):
        collect[:hand_count, copy * parts : (copy + 1) * parts] = sums
        spread[copy * parts : (copy + 1) * parts, :hand_count] = signed.T
    return [table.astype(jnp.bfloat16) for table in (apart, collect, spread)]


def as_column(row):
    size = row.shape[1]
    at = lax.broadcasted_iota(jnp.int32, (size, size), 0) == lax.broadcasted_iota(jnp.int32, (size, size), 1)
    return jnp.sum(jnp.where(at, row.astype(jnp.float32), 0.0), axis=1, keepdims=True)


def pack_kernel(hand_count, count_ref, slots_ref, ranks_ref, live_ref, out_ref):
    wide = up(hand_count, LANE)
    boards = out_ref.shape[0]
    out_ref[:, wide - LANE : wide] = jnp.zeros((boards, LANE), jnp.int32)
    out_ref[:, :hand_count] = ranks_ref[...] + RANK_SPAN * live_ref[...]
    slot = lax.broadcasted_iota(jnp.int32, (1, slots_ref.shape[1]), 1)
    for board in range(boards):
        lines = slots_ref[board : board + 1]
        out_ref[board : board + 1, wide:] = jnp.where(slot < count_ref[board], lines, -1)


def pack(counts, slots, ranks, live):
    hand_count = ranks.shape[1]
    return pl.pallas_call(
        functools.partial(pack_kernel, hand_count),
        out_shape=jax.ShapeDtypeStruct((slots.shape[0], up(hand_count, LANE) + slots.shape[1]), jnp.int32),
        in_specs=[SCALARS] + [WHOLE] * 3,
        out_specs=WHOLE,
        compiler_params=params(4),
        name="pack_boards",
    )(counts, slots, ranks, live)


def fetch_kernel(after_ref, table_ref, out_ref, sem):
    copy = pltpu.make_async_copy(table_ref, out_ref, sem)
    copy.start()
    copy.wait()


def fetch(table, after):
    return pl.pallas_call(
        fetch_kernel,
        out_shape=jax.ShapeDtypeStruct(table.shape, table.dtype),
        in_specs=[WHOLE, pl.BlockSpec(memory_space=pl.ANY)],
        out_specs=WHOLE,
        scratch_shapes=[pltpu.SemaphoreType.DMA],
        compiler_params=params(8),
        name="fetch_table",
        cost_estimate=pl.CostEstimate(flops=0, bytes_accessed=2 * table.size * 2, transcendentals=0),
    )(after, table)


def boards_kernel(hand_count, line_count, base_ref, own_ref, mate_ref, own_kind_ref, mate_kind_ref, *refs, boards_in):
    board_refs, refs = refs[:boards_in], refs[boards_in:]
    apart_ref, collect_ref, spread_ref, own_out, mate_out, column_ref, board_ref, reach_ref = refs
    wide = up(hand_count, LANE)
    deep = apart_ref.shape[0]
    rows = own_ref.shape[0]
    parts = 1 + CARDS
    reach_ref[...] = jnp.zeros_like(reach_ref)
    reach_ref[:rows, :hand_count] = own_ref[...]
    reach_ref[rows:, :hand_count] = mate_ref[...]
    kind = jnp.concatenate([as_column(own_kind_ref[...]), as_column(mate_kind_ref[...])], axis=0)
    row = lax.broadcasted_iota(jnp.int32, (2 * rows, 1), 0)
    within = jnp.where(row < rows, row, row - rows)
    line = jnp.where(row < rows, base_ref[0], base_ref[1]) + within
    line = jnp.where(within < line_count, line, -2)
    lane = lax.broadcasted_iota(jnp.int32, (2 * rows, LANE), 1)
    own_out[...] = jnp.zeros_like(own_out)
    mate_out[...] = jnp.zeros_like(mate_out)
    board_total = 0
    for ref in board_refs:
        board_ref[board_total : board_total + ref.shape[0]] = ref[...]
        board_total += ref.shape[0]

    def add_board(board):
        keys = board_ref[pl.ds(board, 1), :wide]
        slots = board_ref[pl.ds(board, 1), wide:]
        ranks = keys & (RANK_SPAN - 1)
        live = (keys >> (RANK_SPAN.bit_length() - 1)).astype(jnp.float32)
        power = ranks >> (MANTISSA.bit_length() - 1)
        near = jnp.left_shift(1, jnp.minimum(power, 29)).astype(jnp.float32)
        far = jnp.left_shift(1, jnp.maximum(power - 29, 0)).astype(jnp.float32)
        order = ((ranks & (MANTISSA - 1)) + MANTISSA).astype(jnp.float32) * near * far
        column_ref[...] = jnp.transpose(jnp.broadcast_to(order, (LANE, wide)))[:deep].astype(jnp.bfloat16)
        order = order.astype(jnp.bfloat16)
        keep = jnp.max(jnp.where(slots == line, 1.0, 0.0), axis=1, keepdims=True)
        show_keep = jnp.where(kind == 0, keep, 0.0).astype(jnp.bfloat16)
        fold_keep = jnp.where(kind == 0, 0.0, keep).astype(jnp.bfloat16)
        held = reach_ref[...] * live.astype(jnp.bfloat16)
        show_reach = held * show_keep
        fold_reach = held * fold_keep
        sums = jnp.dot(fold_reach, collect_ref[...], preferred_element_type=jnp.float32)
        high = sums.astype(jnp.bfloat16).astype(jnp.float32)
        sums = jnp.where(lane < parts, high, sums - high).astype(jnp.bfloat16)
        one = jnp.bfloat16(1)
        for first, count in tiles(wide, COL_TILE):
            at = slice(first, first + count)
            total = jnp.dot(sums, spread_ref[:, at], preferred_element_type=jnp.float32)
            for top, height in tiles(deep, ROW_TILE):
                down = slice(top, top + height)
                column = jnp.concatenate([column_ref[down]] * (count // LANE), axis=1)
                matrix = jnp.clip(order[:, at] - column, -one, one) * apart_ref[down, at]
                total += jnp.dot(show_reach[:, down], matrix, preferred_element_type=jnp.float32)
            total = (total + fold_reach[:, at].astype(jnp.float32)) * live[:, at]
            own_out[:, at] += total[:rows]
            mate_out[:, at] += total[rows:]

    if board_total <= UNROLL:
        for board in range(board_total):
            add_board(board)
    else:
        pl.loop(0, board_total)(add_board)


def board_sums(hand_count, line_count, base, reach, kinds, boards, apart, collect, spread):
    rows, wide = reach[0].shape[0], up(hand_count, LANE)
    out = jax.ShapeDtypeStruct((rows, wide), jnp.float32)
    total = sum(board.shape[0] for board in boards)
    return pl.pallas_call(
        functools.partial(boards_kernel, hand_count, line_count, boards_in=len(boards)),
        out_shape=(out, out),
        in_specs=[SCALARS] + [WHOLE] * (7 + len(boards)),
        out_specs=(WHOLE, WHOLE),
        scratch_shapes=[
            pltpu.VMEM((apart.shape[0], LANE), jnp.bfloat16),
            pltpu.VMEM((total, boards[0].shape[1]), jnp.int32),
            pltpu.VMEM((2 * rows, wide), jnp.bfloat16),
        ],
        compiler_params=params(32),
        name="board_sums",
        cost_estimate=pl.CostEstimate(flops=4 * total * rows * wide * wide, bytes_accessed=0, transcendentals=0),
    )(base, *reach, *kinds, *boards, apart, collect, spread)


def powers():
    lane = lax.broadcasted_iota(jnp.int32, (1, LANE), 1)
    up_size, down_size = jnp.ones((1, LANE), jnp.float32), jnp.ones((1, LANE), jnp.float32)
    bit = 1
    while bit < LANE:
        chosen = (jnp.abs(lane - LOWEST) & bit) != 0
        up_size = jnp.where(chosen, up_size * 2.0**bit, up_size)
        down_size = jnp.where(chosen, down_size * 0.5**bit, down_size)
        bit *= 2
    return jnp.where(lane < LOWEST, down_size, up_size), jnp.where(lane < LOWEST, up_size, down_size)


def update_kernel(hand_count, scale, own_ref, mate_ref, pot_ref, kind_ref, regret_ref, regret_out, code_out, node_ref):
    pot = as_column(pot_ref[...])
    coef = jnp.where(as_column(kind_ref[...]) == 1, -pot, pot) * scale
    values = (own_ref[:, :hand_count] + mate_ref[:, :hand_count]) * coef
    regrets = regret_ref[...]
    rows = regrets.shape[0]
    even = lax.broadcasted_iota(jnp.int32, (rows, 1), 0) % ACTS == 0

    def both(array):
        other = jnp.where(even, pltpu.roll(array, rows - 1, 0), pltpu.roll(array, 1, 0))
        return array + other

    positive = jnp.maximum(regrets, 0.0)
    strategy = (positive + floor_share) / (both(positive) + ACTS * floor_share)
    node = both(strategy * values)
    regret_out[...] = jnp.maximum(regrets + values - node, 0.0)
    size, flip = powers()
    largest = jnp.max(jnp.abs(node), axis=1, keepdims=True)
    place = jnp.sum(jnp.where(size < largest, 1.0, 0.0), axis=1, keepdims=True)
    lane = lax.broadcasted_iota(jnp.int32, (rows, LANE), 1).astype(jnp.float32)
    gain = jnp.sum(jnp.where(lane == place, flip, 0.0), axis=1, keepdims=True) * STEPS
    codes = node * gain
    for tile, (first, count) in enumerate(tiles(hand_count, LANE)):
        node_ref[tile, :, :count] = codes[:, first : first + count]
        if count < LANE:
            node_ref[tile, :, count:] = jnp.broadcast_to(place, (rows, LANE - count))
        picked = node_ref[tile, pl.ds(0, rows // ACTS, stride=ACTS), :]
        code_out[:, first : first + LANE] = jnp.floor(picked + 0.5).astype(jnp.int32).astype(jnp.int16)


def update(hand_count, scale, own, mate, pots, kinds, regrets):
    rows = regrets.shape[0]
    return pl.pallas_call(
        functools.partial(update_kernel, hand_count, scale),
        out_shape=(
            jax.ShapeDtypeStruct((rows, hand_count), jnp.float32),
            jax.ShapeDtypeStruct((rows // ACTS, up(hand_count, LANE)), jnp.int16),
        ),
        in_specs=[WHOLE] * 5,
        out_specs=(WHOLE, WHOLE),
        scratch_shapes=[pltpu.VMEM((up(hand_count, LANE) // LANE, rows, LANE), jnp.float32)],
        compiler_params=params(8),
        name="regret_update",
    )(own, mate, pots, kinds, regrets)


def chance_kernel(hand_count, *refs):
    code_refs, out_ref = refs[:-1], refs[-1]
    size, _ = powers()
    lane = lax.broadcasted_iota(jnp.int32, (out_ref.shape[0], LANE), 1)

    def value(ref):
        codes = ref[...].astype(jnp.int32)
        place = codes[:, hand_count : hand_count + 1]
        gain = jnp.sum(jnp.where(lane == place, size, 0.0), axis=1, keepdims=True)
        return codes[:, :hand_count].astype(jnp.float32) * (gain * (1.0 / (STEPS * len(code_refs))))

    total = None
    for first, second in zip(code_refs[::2], code_refs[1::2]):
        pair = value(first) + value(second)
        total = pair if total is None else total + pair
    out_ref[...] = total


def chance(hand_count, codes):
    return pl.pallas_call(
        functools.partial(chance_kernel, hand_count),
        out_shape=jax.ShapeDtypeStruct((codes[0].shape[0], hand_count), jnp.float32),
        in_specs=[WHOLE] * len(codes),
        out_specs=WHOLE,
        compiler_params=params(8),
        name="chance_sum",
    )(*codes)


def swap(array, axes, mask):
    return lax.ppermute(array, axes, [(index, index ^ mask) for index in range(lax.axis_size(axes))])


def on_device(
    regrets, opp_reach, pot_size, line_kind, board_lines, board_count, hand_ranks, live_hands
):
    hand_count = opp_reach.shape[2]
    line_count = opp_reach.shape[1]
    group = ("turn", "river")
    group_size = lax.axis_size(group)
    core = lax.axis_size("river")
    board_total = group_size * board_lines.shape[2]
    extra = up(line_count, SUB) - line_count
    apart, collect, spread = [jnp.asarray(table) for table in tables(hand_count)]

    boards = pack(board_count[0, 0], board_lines[0, 0], hand_ranks[0, 0], live_hands[0, 0])
    masks = [mask for mask in range(1, group_size) if not mask & core]
    if len(masks) < 4:
        parts = [boards] + [swap(boards, group, mask) for mask in masks]
    else:
        parts = boards
        for mask in masks:
            if mask & (mask - 1) == 0:
                parts = jnp.concatenate([parts, swap(parts, group, mask)], axis=0)
        parts = [parts]
    reach = jnp.pad(opp_reach[0], ((0, extra), (0, 0)))
    kinds = jnp.pad(line_kind, ((0, 0), (0, extra)))
    pots = jnp.pad(pot_size, ((0, 0), (0, extra)))
    held = jnp.pad(regrets[0], ((0, extra), (0, 0)))
    mate_reach, mate_kinds = swap(reach, group, core), swap(kinds, group, core)
    apart = fetch(apart, boards)
    index = lax.axis_index(group)
    base = jnp.stack([index, index ^ core]).astype(jnp.int32) * line_count
    own, for_mate = board_sums(
        hand_count, line_count, base, (reach, mate_reach), (kinds, mate_kinds), parts, apart, collect, spread
    )
    mate = swap(for_mate, group, core)
    updated, codes = update(hand_count, 1.0 / (board_total * hand_count), own, mate, pots, kinds, held)
    flops = lax.axis_size("flop")
    total = chance(hand_count, [codes] + [swap(codes, "flop", mask) for mask in range(1, flops)])
    return (updated[None, :line_count], total[: line_count // ACTS])


def solution(mesh):
    placed = (
        P("flop", ("turn", "river"), None),
        P("flop", ("turn", "river"), None),
        P("flop", ("turn", "river")),
        P("flop", ("turn", "river")),
        P("flop", "turn", "river", None),
        P("flop", "turn", "river"),
        P("flop", "turn", "river", None),
        P("flop", "turn", "river", None),
    )
    return jax.shard_map(
        on_device,
        mesh=mesh,
        in_specs=placed,
        out_specs=(P("flop", ("turn", "river"), None), P(("turn", "river"), None)),
        check_vma=False,
    )
```

```python
import functools

import jax
import jax.numpy as jnp
import numpy as np
from jax import lax
from jax.experimental import pallas as pl
from jax.experimental.pallas import tpu as pltpu
from jax.sharding import PartitionSpec as P

CARDS = 52
ACTS = 2
LANE = 128
SUB = 32
RANK_SPAN = 8192
MANTISSA = 128
ROW_TILE = 128
COL_TILE = 768
UNROLL = 8
STEPS = 32767.0
LOWEST = 100
FETCH_ROWS = 176
WHOLE = pl.BlockSpec(memory_space=pltpu.VMEM)
SCALARS = pl.BlockSpec(memory_space=pltpu.SMEM)
REMAIN = pl.BlockSpec(memory_space=pltpu.HBM)

floor_share = 0.1


def up(value, unit):
    return -(-value // unit) * unit


def tiles(total, size):
    return [(first, min(size, total - first)) for first in range(0, total, size)]


def params(mebibytes):
    return pltpu.CompilerParams(vmem_limit_bytes=mebibytes << 20)


@functools.cache
def tables(hand_count):
    wide, deep = up(hand_count, LANE), up(hand_count, 16)
    first, second = np.triu_indices(CARDS, 1)
    cards = np.zeros((hand_count, CARDS), np.float32)
    cards[np.arange(hand_count), first] = 1
    cards[np.arange(hand_count), second] = 1
    apart = np.zeros((deep, wide), np.float32)
    apart[:hand_count, :hand_count] = (cards @ cards.T) == 0
    sums = np.concatenate([np.ones((hand_count, 1), np.float32), cards], axis=1)
    parts = sums.shape[1]
    collect = np.zeros((wide, LANE), np.float32)
    spread = np.zeros((LANE, wide), np.float32)
    signed = sums.copy()
    signed[:, 1:] *= -1
    for copy in range(2):
        collect[:hand_count, copy * parts : (copy + 1) * parts] = sums
        spread[copy * parts : (copy + 1) * parts, :hand_count] = signed.T
    return [table.astype(jnp.bfloat16) for table in (apart, collect, spread)]


def as_column(row):
    size = row.shape[1]
    at = lax.broadcasted_iota(jnp.int32, (size, size), 0) == lax.broadcasted_iota(jnp.int32, (size, size), 1)
    return jnp.sum(jnp.where(at, row.astype(jnp.float32), 0.0), axis=1, keepdims=True)


def copy_all(pairs, sems):
    copies = [pltpu.make_async_copy(source, target, sems.at[at]) for at, (source, target) in enumerate(pairs)]
    for copy in copies:
        copy.start()
    for copy in copies:
        copy.wait()


def pack_kernel(hand_count, count_ref, slots_hbm, ranks_hbm, live_hbm, out_ref, slots_ref, ranks_ref, live_ref, sems):
    wide = up(hand_count, LANE)
    boards = out_ref.shape[0]
    copy_all([(slots_hbm, slots_ref), (ranks_hbm, ranks_ref), (live_hbm, live_ref)], sems)
    out_ref[:, wide - LANE : wide] = jnp.zeros((boards, LANE), jnp.int32)
    out_ref[:, :hand_count] = ranks_ref[...] + RANK_SPAN * live_ref[...]
    slot = lax.broadcasted_iota(jnp.int32, (1, slots_ref.shape[1]), 1)
    for board in range(boards):
        lines = slots_ref[board : board + 1]
        out_ref[board : board + 1, wide:] = jnp.where(slot < count_ref[board], lines, -1)


def pack(counts, slots, ranks, live):
    hand_count = ranks.shape[1]
    inputs = (slots, ranks, live)
    return pl.pallas_call(
        functools.partial(pack_kernel, hand_count),
        out_shape=jax.ShapeDtypeStruct((slots.shape[0], up(hand_count, LANE) + slots.shape[1]), jnp.int32),
        in_specs=[SCALARS] + [REMAIN] * 3,
        out_specs=WHOLE,
        scratch_shapes=[pltpu.VMEM(array.shape, array.dtype) for array in inputs] + [pltpu.SemaphoreType.DMA((3,))],
        compiler_params=params(4),
        name="pack_boards",
    )(counts, *inputs)


def fetch_kernel(after_ref, *refs):
    tables_in, tables_out, sems = refs[:3], refs[3:6], refs[6]
    pairs = []
    for source, target in zip(tables_in, tables_out):
        for first, count in tiles(source.shape[0], FETCH_ROWS):
            pairs.append((source.at[pl.ds(first, count)], target.at[pl.ds(first, count)]))
    copy_all(pairs, sems)


def fetch(arrays, after):
    copies = sum(len(tiles(array.shape[0], FETCH_ROWS)) for array in arrays)
    return pl.pallas_call(
        fetch_kernel,
        out_shape=[jax.ShapeDtypeStruct(array.shape, array.dtype) for array in arrays],
        in_specs=[WHOLE] + [REMAIN] * len(arrays),
        out_specs=[WHOLE] * len(arrays),
        scratch_shapes=[pltpu.SemaphoreType.DMA((copies,))],
        compiler_params=params(12),
        name="fetch_tables",
        cost_estimate=pl.CostEstimate(
            flops=0, bytes_accessed=sum(2 * array.nbytes for array in arrays), transcendentals=0
        ),
    )(after, *arrays)


def boards_kernel(hand_count, line_count, base_ref, own_ref, mate_ref, own_kind_ref, mate_kind_ref, *refs, boards_in):
    board_refs, refs = refs[:boards_in], refs[boards_in:]
    apart_ref, collect_ref, spread_ref, own_out, mate_out, column_ref, board_ref, reach_ref = refs
    wide = up(hand_count, LANE)
    deep = apart_ref.shape[0]
    rows = own_ref.shape[0]
    parts = 1 + CARDS
    reach_ref[...] = jnp.zeros_like(reach_ref)
    reach_ref[:rows, :hand_count] = own_ref[...]
    reach_ref[rows:, :hand_count] = mate_ref[...]
    kind = jnp.concatenate([as_column(own_kind_ref[...]), as_column(mate_kind_ref[...])], axis=0)
    row = lax.broadcasted_iota(jnp.int32, (2 * rows, 1), 0)
    within = jnp.where(row < rows, row, row - rows)
    line = jnp.where(row < rows, base_ref[0], base_ref[1]) + within
    line = jnp.where(within < line_count, line, -2)
    lane = lax.broadcasted_iota(jnp.int32, (2 * rows, LANE), 1)
    own_out[...] = jnp.zeros_like(own_out)
    mate_out[...] = jnp.zeros_like(mate_out)
    board_total = 0
    for ref in board_refs:
        board_ref[board_total : board_total + ref.shape[0]] = ref[...]
        board_total += ref.shape[0]

    def add_board(board):
        keys = board_ref[pl.ds(board, 1), :wide]
        slots = board_ref[pl.ds(board, 1), wide:]
        ranks = keys & (RANK_SPAN - 1)
        live = (keys >> (RANK_SPAN.bit_length() - 1)).astype(jnp.float32)
        power = ranks >> (MANTISSA.bit_length() - 1)
        near = jnp.left_shift(1, jnp.minimum(power, 29)).astype(jnp.float32)
        far = jnp.left_shift(1, jnp.maximum(power - 29, 0)).astype(jnp.float32)
        order = ((ranks & (MANTISSA - 1)) + MANTISSA).astype(jnp.float32) * near * far
        column_ref[...] = jnp.transpose(jnp.broadcast_to(order, (LANE, wide)))[:deep].astype(jnp.bfloat16)
        order = order.astype(jnp.bfloat16)
        keep = jnp.max(jnp.where(slots == line, 1.0, 0.0), axis=1, keepdims=True)
        show_keep = jnp.where(kind == 0, keep, 0.0).astype(jnp.bfloat16)
        fold_keep = jnp.where(kind == 0, 0.0, keep).astype(jnp.bfloat16)
        held = reach_ref[...] * live.astype(jnp.bfloat16)
        show_reach = held * show_keep
        fold_reach = held * fold_keep
        sums = jnp.dot(fold_reach, collect_ref[...], preferred_element_type=jnp.float32)
        high = sums.astype(jnp.bfloat16).astype(jnp.float32)
        sums = jnp.where(lane < parts, high, sums - high).astype(jnp.bfloat16)
        one = jnp.bfloat16(1)
        for first, count in tiles(wide, COL_TILE):
            at = slice(first, first + count)
            total = jnp.dot(sums, spread_ref[:, at], preferred_element_type=jnp.float32)
            for top, height in tiles(deep, ROW_TILE):
                down = slice(top, top + height)
                column = jnp.concatenate([column_ref[down]] * (count // LANE), axis=1)
                matrix = jnp.clip(order[:, at] - column, -one, one) * apart_ref[down, at]
                total += jnp.dot(show_reach[:, down], matrix, preferred_element_type=jnp.float32)
            total = (total + fold_reach[:, at].astype(jnp.float32)) * live[:, at]
            own_out[:, at] += total[:rows]
            mate_out[:, at] += total[rows:]

    if board_total <= UNROLL:
        for board in range(board_total):
            add_board(board)
    else:
        pl.loop(0, board_total)(add_board)


def board_sums(hand_count, line_count, base, reach, kinds, boards, apart, collect, spread):
    rows, wide = reach[0].shape[0], up(hand_count, LANE)
    out = jax.ShapeDtypeStruct((rows, wide), jnp.float32)
    total = sum(board.shape[0] for board in boards)
    return pl.pallas_call(
        functools.partial(boards_kernel, hand_count, line_count, boards_in=len(boards)),
        out_shape=(out, out),
        in_specs=[SCALARS] + [WHOLE] * (7 + len(boards)),
        out_specs=(WHOLE, WHOLE),
        scratch_shapes=[
            pltpu.VMEM((apart.shape[0], LANE), jnp.bfloat16),
            pltpu.VMEM((total, boards[0].shape[1]), jnp.int32),
            pltpu.VMEM((2 * rows, wide), jnp.bfloat16),
        ],
        compiler_params=params(32),
        name="board_sums",
        cost_estimate=pl.CostEstimate(flops=4 * total * rows * wide * wide, bytes_accessed=0, transcendentals=0),
    )(base, *reach, *kinds, *boards, apart, collect, spread)


def powers():
    lane = lax.broadcasted_iota(jnp.int32, (1, LANE), 1)
    up_size, down_size = jnp.ones((1, LANE), jnp.float32), jnp.ones((1, LANE), jnp.float32)
    bit = 1
    while bit < LANE:
        chosen = (jnp.abs(lane - LOWEST) & bit) != 0
        up_size = jnp.where(chosen, up_size * 2.0**bit, up_size)
        down_size = jnp.where(chosen, down_size * 0.5**bit, down_size)
        bit *= 2
    return jnp.where(lane < LOWEST, down_size, up_size), jnp.where(lane < LOWEST, up_size, down_size)


def update_kernel(hand_count, scale, own_ref, mate_ref, pot_ref, kind_ref, regret_ref, regret_out, code_out, node_ref):
    pot = as_column(pot_ref[...])
    coef = jnp.where(as_column(kind_ref[...]) == 1, -pot, pot) * scale
    values = (own_ref[:, :hand_count] + mate_ref[:, :hand_count]) * coef
    regrets = regret_ref[...]
    rows = regrets.shape[0]
    even = lax.broadcasted_iota(jnp.int32, (rows, 1), 0) % ACTS == 0

    def both(array):
        other = jnp.where(even, pltpu.roll(array, rows - 1, 0), pltpu.roll(array, 1, 0))
        return array + other

    positive = jnp.maximum(regrets, 0.0)
    strategy = (positive + floor_share) / (both(positive) + ACTS * floor_share)
    node = both(strategy * values)
    regret_out[...] = jnp.maximum(regrets + values - node, 0.0)
    size, flip = powers()
    largest = jnp.max(jnp.abs(node), axis=1, keepdims=True)
    place = jnp.sum(jnp.where(size < largest, 1.0, 0.0), axis=1, keepdims=True)
    lane = lax.broadcasted_iota(jnp.int32, (rows, LANE), 1).astype(jnp.float32)
    gain = jnp.sum(jnp.where(lane == place, flip, 0.0), axis=1, keepdims=True) * STEPS
    codes = node * gain
    for tile, (first, count) in enumerate(tiles(hand_count, LANE)):
        node_ref[tile, :, :count] = codes[:, first : first + count]
        if count < LANE:
            node_ref[tile, :, count:] = jnp.broadcast_to(place, (rows, LANE - count))
        picked = node_ref[tile, pl.ds(0, rows // ACTS, stride=ACTS), :]
        code_out[:, first : first + LANE] = jnp.floor(picked + 0.5).astype(jnp.int32).astype(jnp.int16)


def update(hand_count, scale, own, mate, pots, kinds, regrets):
    rows = regrets.shape[0]
    return pl.pallas_call(
        functools.partial(update_kernel, hand_count, scale),
        out_shape=(
            jax.ShapeDtypeStruct((rows, hand_count), jnp.float32),
            jax.ShapeDtypeStruct((rows // ACTS, up(hand_count, LANE)), jnp.int16),
        ),
        in_specs=[WHOLE] * 5,
        out_specs=(WHOLE, WHOLE),
        scratch_shapes=[pltpu.VMEM((up(hand_count, LANE) // LANE, rows, LANE), jnp.float32)],
        compiler_params=params(8),
        name="regret_update",
    )(own, mate, pots, kinds, regrets)


def chance_kernel(hand_count, *refs):
    code_refs, out_ref = refs[:-1], refs[-1]
    size, _ = powers()
    lane = lax.broadcasted_iota(jnp.int32, (out_ref.shape[0], LANE), 1)

    def value(ref):
        codes = ref[...].astype(jnp.int32)
        place = codes[:, hand_count : hand_count + 1]
        gain = jnp.sum(jnp.where(lane == place, size, 0.0), axis=1, keepdims=True)
        return codes[:, :hand_count].astype(jnp.float32) * (gain * (1.0 / (STEPS * len(code_refs))))

    total = None
    for first, second in zip(code_refs[::2], code_refs[1::2]):
        pair = value(first) + value(second)
        total = pair if total is None else total + pair
    out_ref[...] = total


def chance(hand_count, codes):
    return pl.pallas_call(
        functools.partial(chance_kernel, hand_count),
        out_shape=jax.ShapeDtypeStruct((codes[0].shape[0], hand_count), jnp.float32),
        in_specs=[WHOLE] * len(codes),
        out_specs=WHOLE,
        compiler_params=params(8),
        name="chance_sum",
    )(*codes)


def swap(array, axes, mask):
    return lax.ppermute(array, axes, [(index, index ^ mask) for index in range(lax.axis_size(axes))])


def on_device(
    regrets, opp_reach, pot_size, line_kind, board_lines, board_count, hand_ranks, live_hands
):
    hand_count = opp_reach.shape[2]
    line_count = opp_reach.shape[1]
    group = ("turn", "river")
    group_size = lax.axis_size(group)
    core = lax.axis_size("river")
    board_total = group_size * board_lines.shape[2]
    extra = up(line_count, SUB) - line_count
    boards = pack(board_count[0, 0], board_lines[0, 0], hand_ranks[0, 0], live_hands[0, 0])
    masks = [mask for mask in range(1, group_size) if not mask & core]
    if len(masks) < 4:
        parts = [boards] + [swap(boards, group, mask) for mask in masks]
    else:
        parts = boards
        for mask in masks:
            if mask & (mask - 1) == 0:
                parts = jnp.concatenate([parts, swap(parts, group, mask)], axis=0)
        parts = [parts]
    reach = jnp.pad(opp_reach[0], ((0, extra), (0, 0)))
    kinds = jnp.pad(line_kind, ((0, 0), (0, extra)))
    pots = jnp.pad(pot_size, ((0, 0), (0, extra)))
    held = jnp.pad(regrets[0], ((0, extra), (0, 0)))
    mate_reach, mate_kinds = swap(reach, group, core), swap(kinds, group, core)
    held_tables = fetch([jnp.asarray(table) for table in tables(hand_count)], boards)
    index = lax.axis_index(group)
    base = jnp.stack([index, index ^ core]).astype(jnp.int32) * line_count
    own, for_mate = board_sums(
        hand_count, line_count, base, (reach, mate_reach), (kinds, mate_kinds), parts, *held_tables
    )
    mate = swap(for_mate, group, core)
    updated, codes = update(hand_count, 1.0 / (board_total * hand_count), own, mate, pots, kinds, held)
    flops = lax.axis_size("flop")
    arrived = {mask: swap(codes, "flop", mask) for mask in (flops - 1, *range(1, flops - 1))}
    total = chance(hand_count, [codes] + [arrived[mask] for mask in range(1, flops)])
    return (updated[None, :line_count], total[: line_count // ACTS])


def solution(mesh):
    placed = (
        P("flop", ("turn", "river"), None),
        P("flop", ("turn", "river"), None),
        P("flop", ("turn", "river")),
        P("flop", ("turn", "river")),
        P("flop", "turn", "river", None),
        P("flop", "turn", "river"),
        P("flop", "turn", "river", None),
        P("flop", "turn", "river", None),
    )
    return jax.shard_map(
        on_device,
        mesh=mesh,
        in_specs=placed,
        out_specs=(P("flop", ("turn", "river"), None), P(("turn", "river"), None)),
        check_vma=False,
    )
```

```python
import functools

import jax
import jax.numpy as jnp
import numpy as np
from jax import lax
from jax.experimental import pallas as pl
from jax.experimental.pallas import tpu as pltpu
from jax.sharding import PartitionSpec as P

CARDS = 52
ACTS = 2
LANE = 128
SUB = 32
RANK_SPAN = 8192
MANTISSA = 128
ROW_TILE = 128
COL_TILE = 768
UNROLL = 8
STEPS = 32767.0
LOWEST = 100
TABLE_TYPE = jnp.int8
WHOLE = pl.BlockSpec(memory_space=pltpu.VMEM)

floor_share = 0.1


def up(value, unit):
    return -(-value // unit) * unit


def tiles(total, size):
    return [(first, min(size, total - first)) for first in range(0, total, size)]


def params(mebibytes):
    return pltpu.CompilerParams(vmem_limit_bytes=mebibytes << 20)


@functools.cache
def table(hand_count):
    wide, deep = up(hand_count, LANE), up(hand_count, 16)
    first, second = np.triu_indices(CARDS, 1)
    cards = np.zeros((hand_count, CARDS), np.float32)
    cards[np.arange(hand_count), first] = 1
    cards[np.arange(hand_count), second] = 1
    apart = np.zeros((deep, wide), np.float32)
    apart[:hand_count, :hand_count] = (cards @ cards.T) == 0
    sums = np.zeros((LANE, wide), np.float32)
    for first in (0, 1 + CARDS):
        sums[first, :hand_count] = 1
        sums[first + 1 : first + 1 + CARDS, :hand_count] = cards.T
    return np.concatenate([apart, sums]).astype(TABLE_TYPE)


def as_column(row):
    size = row.shape[1]
    at = lax.broadcasted_iota(jnp.int32, (size, size), 0) == lax.broadcasted_iota(jnp.int32, (size, size), 1)
    return jnp.sum(jnp.where(at, row.astype(jnp.float32), 0.0), axis=1, keepdims=True)


def copy_all(pairs, sems):
    copies = [pltpu.make_async_copy(source, target, sems.at[at]) for at, (source, target) in enumerate(pairs)]
    for copy in copies:
        copy.start()
    for copy in copies:
        copy.wait()


def bases_kernel(line_count, core, out_ref):
    index = lax.axis_index("turn") * lax.axis_size("river") + lax.axis_index("river")
    lane = lax.broadcasted_iota(jnp.int32, out_ref.shape, 1)
    line = jnp.where(lane == LANE // 2, index, index ^ core) * line_count
    out_ref[...] = jnp.where((lane == LANE // 2) | (lane == LANE // 2 + 1), line, 0)


def first_lines(line_count, core):
    return pl.pallas_call(
        functools.partial(bases_kernel, line_count, core),
        out_shape=jax.ShapeDtypeStruct((1, LANE), jnp.int32),
        out_specs=WHOLE,
        compiler_params=params(4),
        name="first_lines",
        cost_estimate=pl.CostEstimate(flops=20 * 10**9, bytes_accessed=0, transcendentals=0),
    )()


def pack(counts, slots, ranks, live, kinds, bases):
    hand_count, slot_count, boards = ranks.shape[1], slots.shape[1], ranks.shape[0]
    wide = up(hand_count, LANE)

    def place(array, first):
        after = wide + slot_count + LANE - first - array.shape[1]
        return jnp.pad(array, ((0, boards - array.shape[0]), (first, after)))

    packed = place(ranks, 0) + RANK_SPAN * place(live, 0) + place(slots, wide) + place(kinds, wide + slot_count)
    packed += place(bases, wide + slot_count)
    lane = lax.broadcasted_iota(jnp.int32, packed.shape, 1)
    return jnp.where(lane == wide - 1, lax.broadcast_in_dim(counts, packed.shape, (0,)), packed)


def unpack_kernel(after_ref, table_ref, apart_ref, collect_ref, spread_ref):
    deep = apart_ref.shape[0]
    apart_ref[...] = table_ref[:deep].astype(jnp.bfloat16)
    cards = table_ref[deep:].astype(jnp.float32)
    spread_ref[...] = cards.astype(jnp.bfloat16)
    row = lax.broadcasted_iota(jnp.int32, (LANE, 1), 0)
    signed = jnp.where((row == 0) | (row == 1 + CARDS), cards, -cards)
    collect_ref[...] = jnp.transpose(signed).astype(jnp.bfloat16)


def unpack(table, after):
    deep, wide = table.shape[0] - LANE, table.shape[1]
    return pl.pallas_call(
        unpack_kernel,
        out_shape=[jax.ShapeDtypeStruct(shape, jnp.bfloat16) for shape in ((deep, wide), (wide, LANE), (LANE, wide))],
        in_specs=[WHOLE] * 2,
        out_specs=[WHOLE] * 3,
        compiler_params=params(12),
        name="unpack_tables",
        cost_estimate=pl.CostEstimate(flops=4 * 10**9, bytes_accessed=3 * table.size, transcendentals=0),
    )(after, table)


def lines_kernel(hand_count, line_count, own_ref, mate_ref, mate_kind_ref, packed_ref, reach_ref, line_ref):
    rows = own_ref.shape[0]
    first = packed_ref.shape[1] - LANE
    base = packed_ref[:1, first + LANE // 2 : first + LANE // 2 + 2]
    reach_ref[...] = jnp.zeros_like(reach_ref)
    reach_ref[:rows, :hand_count] = own_ref[...]
    reach_ref[rows:, :hand_count] = mate_ref[...]
    own_kind = as_column(packed_ref[:1, first : first + rows])
    kind = jnp.concatenate([own_kind, as_column(mate_kind_ref[...])], axis=0)
    row = lax.broadcasted_iota(jnp.int32, (2 * rows, 1), 0)
    within = jnp.where(row < rows, row, row - rows)
    line = jnp.where(row < rows, base[:, :1], base[:, 1:]) + within
    line = jnp.where(within < line_count, line, -2)
    lane = lax.broadcasted_iota(jnp.int32, line_ref.shape, 1)
    line_ref[...] = jnp.where(lane == 0, line, kind.astype(jnp.int32))


def first_kernel(hand_count, line_count, own_ref, mate_ref, mate_kind_ref, *refs):
    tables, (packed_ref, own_out, mate_out, reach_ref, line_ref), scratch = refs[:3], refs[3:8], refs[8:]
    lines_kernel(hand_count, line_count, own_ref, mate_ref, mate_kind_ref, packed_ref, reach_ref, line_ref)
    own_out[...] = jnp.zeros_like(own_out)
    mate_out[...] = jnp.zeros_like(mate_out)
    add_boards(reach_ref, line_ref, *tables, packed_ref, own_out, mate_out, *scratch)


def second_kernel(reach_ref, line_ref, *refs):
    tables, (packed_ref, own_ref, mate_ref, own_out, mate_out), scratch = refs[:3], refs[3:8], refs[8:]
    own_out[...] = own_ref[...]
    mate_out[...] = mate_ref[...]
    add_boards(reach_ref, line_ref, *tables, packed_ref, own_out, mate_out, *scratch)


def add_boards(
    reach_ref, line_ref, apart_ref, collect_ref, spread_ref, packed_ref, own_out, mate_out, column_ref, board_ref
):
    wide, deep = apart_ref.shape[1], apart_ref.shape[0]
    rows = own_out.shape[0]
    parts = 1 + CARDS
    line, kind = line_ref[:, :1], line_ref[:, 1:2]
    lane = lax.broadcasted_iota(jnp.int32, (2 * rows, LANE), 1)
    board_total = packed_ref.shape[0]
    end = packed_ref.shape[1] - LANE
    slot = lax.broadcasted_iota(jnp.int32, (board_total, end - wide), 1)
    board_ref[:, :wide] = packed_ref[:, :wide]
    board_ref[:, wide:] = jnp.where(slot < packed_ref[:, wide - 1 : wide], packed_ref[:, wide:end], -1)

    def add_board(board):
        keys = board_ref[pl.ds(board, 1), :wide]
        slots = board_ref[pl.ds(board, 1), wide:]
        ranks = keys & (RANK_SPAN - 1)
        live = (keys >> (RANK_SPAN.bit_length() - 1)).astype(jnp.float32)
        power = ranks >> (MANTISSA.bit_length() - 1)
        near = jnp.left_shift(1, jnp.minimum(power, 29)).astype(jnp.float32)
        far = jnp.left_shift(1, jnp.maximum(power - 29, 0)).astype(jnp.float32)
        order = ((ranks & (MANTISSA - 1)) + MANTISSA).astype(jnp.float32) * near * far
        column_ref[...] = jnp.transpose(jnp.broadcast_to(order, (LANE, wide)))[:deep].astype(jnp.bfloat16)
        order = order.astype(jnp.bfloat16)
        keep = jnp.max(jnp.where(slots == line, 1.0, 0.0), axis=1, keepdims=True)
        show_keep = jnp.where(kind == 0, keep, 0.0).astype(jnp.bfloat16)
        fold_keep = jnp.where(kind == 0, 0.0, keep).astype(jnp.bfloat16)
        held = reach_ref[...] * live.astype(jnp.bfloat16)
        show_reach = held * show_keep
        fold_reach = held * fold_keep
        sums = jnp.dot(fold_reach, collect_ref[...], preferred_element_type=jnp.float32)
        high = sums.astype(jnp.bfloat16).astype(jnp.float32)
        sums = jnp.where(lane < parts, high, sums - high).astype(jnp.bfloat16)
        one = jnp.bfloat16(1)
        for first, count in tiles(wide, COL_TILE):
            at = slice(first, first + count)
            total = jnp.dot(sums, spread_ref[:, at], preferred_element_type=jnp.float32)
            for top, height in tiles(deep, ROW_TILE):
                down = slice(top, top + height)
                column = jnp.concatenate([column_ref[down]] * (count // LANE), axis=1)
                matrix = jnp.clip(order[:, at] - column, -one, one) * apart_ref[down, at]
                total += jnp.dot(show_reach[:, down], matrix, preferred_element_type=jnp.float32)
            total = (total + fold_reach[:, at].astype(jnp.float32)) * live[:, at]
            own_out[:, at] += total[:rows]
            mate_out[:, at] += total[rows:]

    if board_total <= UNROLL:
        for board in range(board_total):
            add_board(board)
    else:
        pl.loop(0, board_total)(add_board)


def board_sums(kernel, name, rows, inputs, tables, boards, sums=(), more=()):
    deep, wide = tables[0].shape
    out = [jax.ShapeDtypeStruct((rows, wide), jnp.float32)] * 2 + list(more)
    return pl.pallas_call(
        kernel,
        out_shape=out,
        in_specs=[WHOLE] * (len(inputs) + len(tables) + 1 + len(sums)),
        out_specs=[WHOLE] * len(out),
        scratch_shapes=[
            pltpu.VMEM((deep, LANE), jnp.bfloat16),
            pltpu.VMEM((boards.shape[0], boards.shape[1] - LANE), jnp.int32),
        ],
        compiler_params=params(32),
        name=name,
        cost_estimate=pl.CostEstimate(
            flops=4 * boards.shape[0] * rows * wide * wide, bytes_accessed=0, transcendentals=0
        ),
    )(*inputs, *tables, boards, *sums)


def powers():
    lane = lax.broadcasted_iota(jnp.int32, (1, LANE), 1)
    up_size, down_size = jnp.ones((1, LANE), jnp.float32), jnp.ones((1, LANE), jnp.float32)
    bit = 1
    while bit < LANE:
        chosen = (jnp.abs(lane - LOWEST) & bit) != 0
        up_size = jnp.where(chosen, up_size * 2.0**bit, up_size)
        down_size = jnp.where(chosen, down_size * 0.5**bit, down_size)
        bit *= 2
    return jnp.where(lane < LOWEST, down_size, up_size), jnp.where(lane < LOWEST, up_size, down_size)


def update_kernel(hand_count, scale, own_ref, mate_ref, pot_ref, kind_ref, regret_ref, regret_out, code_out, node_ref):
    pot = as_column(pot_ref[...])
    coef = jnp.where(as_column(kind_ref[...]) == 1, -pot, pot) * scale
    values = (own_ref[:, :hand_count] + mate_ref[:, :hand_count]) * coef
    regrets = regret_ref[...]
    rows = regrets.shape[0]
    even = lax.broadcasted_iota(jnp.int32, (rows, 1), 0) % ACTS == 0

    def both(array):
        other = jnp.where(even, pltpu.roll(array, rows - 1, 0), pltpu.roll(array, 1, 0))
        return array + other

    positive = jnp.maximum(regrets, 0.0)
    strategy = (positive + floor_share) / (both(positive) + ACTS * floor_share)
    node = both(strategy * values)
    regret_out[...] = jnp.maximum(regrets + values - node, 0.0)
    size, flip = powers()
    largest = jnp.max(jnp.abs(node), axis=1, keepdims=True)
    place = jnp.sum(jnp.where(size < largest, 1.0, 0.0), axis=1, keepdims=True)
    lane = lax.broadcasted_iota(jnp.int32, (rows, LANE), 1).astype(jnp.float32)
    gain = jnp.sum(jnp.where(lane == place, flip, 0.0), axis=1, keepdims=True) * STEPS
    codes = node * gain
    for tile, (first, count) in enumerate(tiles(hand_count, LANE)):
        node_ref[tile, :, :count] = codes[:, first : first + count]
        if count < LANE:
            node_ref[tile, :, count:] = jnp.broadcast_to(place, (rows, LANE - count))
        picked = node_ref[tile, pl.ds(0, rows // ACTS, stride=ACTS), :]
        code_out[:, first : first + LANE] = jnp.floor(picked + 0.5).astype(jnp.int32).astype(jnp.int16)


def update(hand_count, scale, own, mate, pots, kinds, regrets):
    rows = regrets.shape[0]
    return pl.pallas_call(
        functools.partial(update_kernel, hand_count, scale),
        out_shape=(
            jax.ShapeDtypeStruct((rows, hand_count), jnp.float32),
            jax.ShapeDtypeStruct((rows // ACTS, up(hand_count, LANE)), jnp.int16),
        ),
        in_specs=[WHOLE] * 5,
        out_specs=(WHOLE, WHOLE),
        scratch_shapes=[pltpu.VMEM((up(hand_count, LANE) // LANE, rows, LANE), jnp.float32)],
        compiler_params=params(8),
        name="regret_update",
    )(own, mate, pots, kinds, regrets)


def chance_kernel(hand_count, *refs):
    code_refs, out_ref = refs[:-1], refs[-1]
    size, _ = powers()
    lane = lax.broadcasted_iota(jnp.int32, (out_ref.shape[0], LANE), 1)

    def value(ref):
        codes = ref[...].astype(jnp.int32)
        place = codes[:, hand_count : hand_count + 1]
        gain = jnp.sum(jnp.where(lane == place, size, 0.0), axis=1, keepdims=True)
        return codes[:, :hand_count].astype(jnp.float32) * (gain * (1.0 / (STEPS * len(code_refs))))

    total = None
    for first, second in zip(code_refs[::2], code_refs[1::2]):
        pair = value(first) + value(second)
        total = pair if total is None else total + pair
    out_ref[...] = total


def chance(hand_count, codes):
    return pl.pallas_call(
        functools.partial(chance_kernel, hand_count),
        out_shape=jax.ShapeDtypeStruct((codes[0].shape[0], hand_count), jnp.float32),
        in_specs=[WHOLE] * len(codes),
        out_specs=WHOLE,
        compiler_params=params(8),
        name="chance_sum",
    )(*codes)


def swap(array, axes, mask):
    return lax.ppermute(array, axes, [(index, index ^ mask) for index in range(lax.axis_size(axes))])


def on_device(
    regrets, opp_reach, pot_size, line_kind, board_lines, board_count, hand_ranks, live_hands
):
    hand_count = opp_reach.shape[2]
    line_count = opp_reach.shape[1]
    group = ("turn", "river")
    group_size = lax.axis_size(group)
    core = lax.axis_size("river")
    board_total = group_size * board_lines.shape[2]
    extra = up(line_count, SUB) - line_count
    bases = first_lines(line_count, core)
    kinds = jnp.pad(line_kind, ((0, 0), (0, extra)))
    boards = pack(board_count[0, 0], board_lines[0, 0], hand_ranks[0, 0], live_hands[0, 0], kinds, bases)
    held, arrived = boards, boards
    for bit in range(group_size.bit_length() - 1):
        mask = 1 << bit
        if mask != core:
            held = boards if mask == 1 else jnp.concatenate([held, arrived], axis=0)
            arrived = swap(held, group, mask)
    reach = jnp.pad(opp_reach[0], ((0, extra), (0, 0)))
    pots = jnp.pad(pot_size, ((0, 0), (0, extra)))
    old_regrets = jnp.pad(regrets[0], ((0, extra), (0, 0)))
    mate_reach, mate_kinds = swap(reach, group, core), swap(kinds, group, core)
    held_tables = unpack(jnp.asarray(table(hand_count)), boards)
    rows, wide = reach.shape[0], up(hand_count, LANE)
    own, for_mate, all_reach, lines = board_sums(
        functools.partial(first_kernel, hand_count, line_count),
        "first_boards",
        rows,
        (reach, mate_reach, mate_kinds),
        held_tables,
        held,
        more=(
            jax.ShapeDtypeStruct((2 * rows, wide), jnp.bfloat16),
            jax.ShapeDtypeStruct((2 * rows, LANE), jnp.int32),
        ),
    )
    own, for_mate = board_sums(
        second_kernel, "second_boards", rows, (all_reach, lines), held_tables, arrived, (own, for_mate)
    )
    mate = swap(for_mate, group, core)
    updated, codes = update(hand_count, 1.0 / (board_total * hand_count), own, mate, pots, kinds, old_regrets)
    flops = lax.axis_size("flop")
    arrived = {mask: swap(codes, "flop", mask) for mask in (flops - 1, *range(1, flops - 1))}
    total = chance(hand_count, [codes] + [arrived[mask] for mask in range(1, flops)])
    return (updated[None, :line_count], total[: line_count // ACTS])


def solution(mesh):
    placed = (
        P("flop", ("turn", "river"), None),
        P("flop", ("turn", "river"), None),
        P("flop", ("turn", "river")),
        P("flop", ("turn", "river")),
        P("flop", "turn", "river", None),
        P("flop", "turn", "river"),
        P("flop", "turn", "river", None),
        P("flop", "turn", "river", None),
    )
    return jax.shard_map(
        on_device,
        mesh=mesh,
        in_specs=placed,
        out_specs=(P("flop", ("turn", "river"), None), P(("turn", "river"), None)),
        check_vma=False,
    )
```

```python
import functools

import jax
import jax.numpy as jnp
import numpy as np
from jax import lax
from jax.experimental import pallas as pl
from jax.experimental.pallas import tpu as pltpu
from jax.sharding import PartitionSpec as P

CARDS = 52
ACTS = 2
LANE = 128
SUB = 32
RANK_SPAN = 8192
MANTISSA = 128
ROW_TILE = 128
COL_TILE = 1408
UNROLL = 8
STEPS = 32767.0
LOWEST = 100
TABLE_TYPE = jnp.int8
WHOLE = pl.BlockSpec(memory_space=pltpu.VMEM)

floor_share = 0.1


def up(value, unit):
    return -(-value // unit) * unit


def tiles(total, size):
    return [(first, min(size, total - first)) for first in range(0, total, size)]


def params(mebibytes):
    return pltpu.CompilerParams(vmem_limit_bytes=mebibytes << 20)


@functools.cache
def table(hand_count):
    wide, deep = up(hand_count, LANE), up(hand_count, 16)
    first, second = np.triu_indices(CARDS, 1)
    cards = np.zeros((hand_count, CARDS), np.float32)
    cards[np.arange(hand_count), first] = 1
    cards[np.arange(hand_count), second] = 1
    apart = np.zeros((deep, wide), np.float32)
    apart[:hand_count, :hand_count] = (cards @ cards.T) == 0
    sums = np.zeros((LANE, wide), np.float32)
    for first in (0, 1 + CARDS):
        sums[first, :hand_count] = 1
        sums[first + 1 : first + 1 + CARDS, :hand_count] = cards.T
    return np.concatenate([apart, sums]).astype(TABLE_TYPE)


def as_column(row):
    size = row.shape[1]
    at = lax.broadcasted_iota(jnp.int32, (size, size), 0) == lax.broadcasted_iota(jnp.int32, (size, size), 1)
    return jnp.sum(jnp.where(at, row.astype(jnp.float32), 0.0), axis=1, keepdims=True)


def copy_all(pairs, sems):
    copies = [pltpu.make_async_copy(source, target, sems.at[at]) for at, (source, target) in enumerate(pairs)]
    for copy in copies:
        copy.start()
    for copy in copies:
        copy.wait()


def bases_kernel(line_count, core, out_ref):
    index = lax.axis_index("turn") * lax.axis_size("river") + lax.axis_index("river")
    lane = lax.broadcasted_iota(jnp.int32, out_ref.shape, 1)
    line = jnp.where(lane == LANE // 2, index, index ^ core) * line_count
    out_ref[...] = jnp.where((lane == LANE // 2) | (lane == LANE // 2 + 1), line, 0)


def first_lines(line_count, core):
    return pl.pallas_call(
        functools.partial(bases_kernel, line_count, core),
        out_shape=jax.ShapeDtypeStruct((1, LANE), jnp.int32),
        out_specs=WHOLE,
        compiler_params=params(4),
        name="first_lines",
        cost_estimate=pl.CostEstimate(flops=20 * 10**9, bytes_accessed=0, transcendentals=0),
    )()


def pack(counts, slots, ranks, live, kinds, bases):
    hand_count, slot_count, boards = ranks.shape[1], slots.shape[1], ranks.shape[0]
    wide = up(hand_count, LANE)

    def place(array, first):
        after = wide + slot_count + LANE - first - array.shape[1]
        return jnp.pad(array, ((0, boards - array.shape[0]), (first, after)))

    packed = place(ranks, 0) + RANK_SPAN * place(live, 0) + place(slots, wide) + place(kinds, wide + slot_count)
    packed += place(bases, wide + slot_count)
    lane = lax.broadcasted_iota(jnp.int32, packed.shape, 1)
    return jnp.where(lane == wide - 1, lax.broadcast_in_dim(counts, packed.shape, (0,)), packed)


def unpack_kernel(after_ref, table_ref, apart_ref, collect_ref, spread_ref):
    deep = apart_ref.shape[0]
    apart_ref[...] = table_ref[:deep].astype(jnp.bfloat16)
    cards = table_ref[deep:].astype(jnp.float32)
    spread_ref[...] = cards.astype(jnp.bfloat16)
    row = lax.broadcasted_iota(jnp.int32, (LANE, 1), 0)
    signed = jnp.where((row == 0) | (row == 1 + CARDS), cards, -cards)
    collect_ref[...] = jnp.transpose(signed).astype(jnp.bfloat16)


def unpack(table, after):
    deep, wide = table.shape[0] - LANE, table.shape[1]
    return pl.pallas_call(
        unpack_kernel,
        out_shape=[jax.ShapeDtypeStruct(shape, jnp.bfloat16) for shape in ((deep, wide), (wide, LANE), (LANE, wide))],
        in_specs=[WHOLE] * 2,
        out_specs=[WHOLE] * 3,
        compiler_params=params(12),
        name="unpack_tables",
        cost_estimate=pl.CostEstimate(flops=4 * 10**9, bytes_accessed=3 * table.size, transcendentals=0),
    )(after, table)


def lines_kernel(hand_count, line_count, own_ref, mate_ref, mate_kind_ref, packed_ref, reach_ref, line_ref):
    rows = own_ref.shape[0]
    first = packed_ref.shape[1] - LANE
    base = packed_ref[:1, first + LANE // 2 : first + LANE // 2 + 2]
    reach_ref[...] = jnp.zeros_like(reach_ref)
    reach_ref[:rows, :hand_count] = own_ref[...]
    reach_ref[rows:, :hand_count] = mate_ref[...]
    own_kind = as_column(packed_ref[:1, first : first + rows])
    kind = jnp.concatenate([own_kind, as_column(mate_kind_ref[...])], axis=0)
    row = lax.broadcasted_iota(jnp.int32, (2 * rows, 1), 0)
    within = jnp.where(row < rows, row, row - rows)
    line = jnp.where(row < rows, base[:, :1], base[:, 1:]) + within
    line = jnp.where(within < line_count, line, -2)
    lane = lax.broadcasted_iota(jnp.int32, line_ref.shape, 1)
    line_ref[...] = jnp.where(lane == 0, line, kind.astype(jnp.int32))


def first_kernel(hand_count, line_count, own_ref, mate_ref, mate_kind_ref, *refs):
    tables, (packed_ref, own_out, mate_out, reach_ref, line_ref, same_ref), scratch = refs[:3], refs[3:9], refs[9:]
    same_ref[...] = packed_ref[...]
    lines_kernel(hand_count, line_count, own_ref, mate_ref, mate_kind_ref, packed_ref, reach_ref, line_ref)
    own_out[...] = jnp.zeros_like(own_out)
    mate_out[...] = jnp.zeros_like(mate_out)
    add_boards(reach_ref, line_ref, *tables, packed_ref, own_out, mate_out, *scratch)


def more_kernel(reach_ref, line_ref, *refs):
    tables, (packed_ref, own_ref, mate_ref, own_out, mate_out), scratch = refs[:3], refs[3:8], refs[8:]
    own_out[...] = own_ref[...]
    mate_out[...] = mate_ref[...]
    add_boards(reach_ref, line_ref, *tables, packed_ref, own_out, mate_out, *scratch)


def add_boards(
    reach_ref, line_ref, apart_ref, collect_ref, spread_ref, packed_ref, own_out, mate_out, column_ref, board_ref
):
    wide, deep = apart_ref.shape[1], apart_ref.shape[0]
    rows = own_out.shape[0]
    parts = 1 + CARDS
    line, kind = line_ref[:, :1], line_ref[:, 1:2]
    lane = lax.broadcasted_iota(jnp.int32, (2 * rows, LANE), 1)
    board_total = packed_ref.shape[0]
    end = packed_ref.shape[1] - LANE
    slot = lax.broadcasted_iota(jnp.int32, (board_total, end - wide), 1)
    board_ref[:, :wide] = packed_ref[:, :wide]
    board_ref[:, wide:] = jnp.where(slot < packed_ref[:, wide - 1 : wide], packed_ref[:, wide:end], -1)

    def add_board(board):
        keys = board_ref[pl.ds(board, 1), :wide]
        slots = board_ref[pl.ds(board, 1), wide:]
        ranks = keys & (RANK_SPAN - 1)
        live = (keys >> (RANK_SPAN.bit_length() - 1)).astype(jnp.float32)
        power = ranks >> (MANTISSA.bit_length() - 1)
        near = jnp.left_shift(1, jnp.minimum(power, 29)).astype(jnp.float32)
        far = jnp.left_shift(1, jnp.maximum(power - 29, 0)).astype(jnp.float32)
        order = ((ranks & (MANTISSA - 1)) + MANTISSA).astype(jnp.float32) * near * far
        column_ref[...] = jnp.transpose(jnp.broadcast_to(order, (LANE, wide)))[:deep].astype(jnp.bfloat16)
        order = order.astype(jnp.bfloat16)
        keep = jnp.max(jnp.where(slots == line, 1.0, 0.0), axis=1, keepdims=True)
        show_keep = jnp.where(kind == 0, keep, 0.0).astype(jnp.bfloat16)
        fold_keep = jnp.where(kind == 0, 0.0, keep).astype(jnp.bfloat16)
        held = reach_ref[...] * live.astype(jnp.bfloat16)
        show_reach = held * show_keep
        fold_reach = held * fold_keep
        sums = jnp.dot(fold_reach, collect_ref[...], preferred_element_type=jnp.float32)
        high = sums.astype(jnp.bfloat16).astype(jnp.float32)
        sums = jnp.where(lane < parts, high, sums - high).astype(jnp.bfloat16)
        one = jnp.bfloat16(1)
        for first, count in tiles(wide, COL_TILE):
            at = slice(first, first + count)
            total = 0.0
            for top, height in tiles(deep, ROW_TILE):
                down = slice(top, top + height)
                column = jnp.concatenate([column_ref[down]] * (count // LANE), axis=1)
                matrix = jnp.clip(order[:, at] - column, -one, one) * apart_ref[down, at]
                total += jnp.dot(show_reach[:, down], matrix, preferred_element_type=jnp.float32)
            total += jnp.dot(sums, spread_ref[:, at], preferred_element_type=jnp.float32)
            total = (total + fold_reach[:, at].astype(jnp.float32)) * live[:, at]
            own_out[:, at] += total[:rows]
            mate_out[:, at] += total[rows:]

    if board_total <= UNROLL:
        for board in range(board_total):
            add_board(board)
    else:
        pl.loop(0, board_total)(add_board)


def board_sums(kernel, name, rows, inputs, tables, boards, sums=(), more=()):
    deep, wide = tables[0].shape
    out = [jax.ShapeDtypeStruct((rows, wide), jnp.float32)] * 2 + list(more)
    return pl.pallas_call(
        kernel,
        out_shape=out,
        in_specs=[WHOLE] * (len(inputs) + len(tables) + 1 + len(sums)),
        out_specs=[WHOLE] * len(out),
        scratch_shapes=[
            pltpu.VMEM((deep, LANE), jnp.bfloat16),
            pltpu.VMEM((boards.shape[0], boards.shape[1] - LANE), jnp.int32),
        ],
        compiler_params=params(32),
        name=name,
        cost_estimate=pl.CostEstimate(
            flops=4 * boards.shape[0] * rows * wide * wide, bytes_accessed=0, transcendentals=0
        ),
    )(*inputs, *tables, boards, *sums)


def powers():
    lane = lax.broadcasted_iota(jnp.int32, (1, LANE), 1)
    up_size, down_size = jnp.ones((1, LANE), jnp.float32), jnp.ones((1, LANE), jnp.float32)
    bit = 1
    while bit < LANE:
        chosen = (jnp.abs(lane - LOWEST) & bit) != 0
        up_size = jnp.where(chosen, up_size * 2.0**bit, up_size)
        down_size = jnp.where(chosen, down_size * 0.5**bit, down_size)
        bit *= 2
    return jnp.where(lane < LOWEST, down_size, up_size), jnp.where(lane < LOWEST, up_size, down_size)


def decide(hand_count, scale, own_ref, mate_ref, pot_ref, kind_ref, regret_ref):
    pot = as_column(pot_ref[...])
    coef = jnp.where(as_column(kind_ref[...]) == 1, -pot, pot) * scale
    values = (own_ref[:, :hand_count] + mate_ref[:, :hand_count]) * coef
    regrets = regret_ref[...]
    rows = regrets.shape[0]
    even = lax.broadcasted_iota(jnp.int32, (rows, 1), 0) % ACTS == 0

    def both(array):
        other = jnp.where(even, pltpu.roll(array, rows - 1, 0), pltpu.roll(array, 1, 0))
        return array + other

    positive = jnp.maximum(regrets, 0.0)
    strategy = (positive + floor_share) / (both(positive) + ACTS * floor_share)
    return regrets, values, both(strategy * values)


def regrets_kernel(hand_count, scale, *refs):
    regrets, values, node = decide(hand_count, scale, *refs[:-1])
    refs[-1][...] = jnp.maximum(regrets + values - node, 0.0)


def codes_kernel(hand_count, scale, *refs):
    *inputs, code_out, node_ref = refs
    _, _, node = decide(hand_count, scale, *inputs)
    rows = node.shape[0]
    size, flip = powers()
    largest = jnp.max(jnp.abs(node), axis=1, keepdims=True)
    place = jnp.sum(jnp.where(size < largest, 1.0, 0.0), axis=1, keepdims=True)
    lane = lax.broadcasted_iota(jnp.int32, (rows, LANE), 1).astype(jnp.float32)
    gain = jnp.sum(jnp.where(lane == place, flip, 0.0), axis=1, keepdims=True) * STEPS
    codes = node * gain
    for tile, (first, count) in enumerate(tiles(hand_count, LANE)):
        node_ref[tile, :, :count] = codes[:, first : first + count]
        if count < LANE:
            node_ref[tile, :, count:] = jnp.broadcast_to(place, (rows, LANE - count))
        picked = node_ref[tile, pl.ds(0, rows // ACTS, stride=ACTS), :]
        code_out[:, first : first + LANE] = jnp.floor(picked + 0.5).astype(jnp.int32).astype(jnp.int16)


def decision_call(kernel, name, hand_count, scale, out_shape, inputs, scratch=()):
    return pl.pallas_call(
        functools.partial(kernel, hand_count, scale),
        out_shape=out_shape,
        in_specs=[WHOLE] * len(inputs),
        out_specs=WHOLE,
        scratch_shapes=scratch,
        compiler_params=params(8),
        name=name,
    )(*inputs)


def chance_kernel(hand_count, order, *refs):
    code_refs, out_ref = refs[:-1], refs[-1]
    size, _ = powers()
    lane = lax.broadcasted_iota(jnp.int32, (out_ref.shape[0], LANE), 1)

    def value(ref):
        codes = ref[...].astype(jnp.int32)
        place = codes[:, hand_count : hand_count + 1]
        gain = jnp.sum(jnp.where(lane == place, size, 0.0), axis=1, keepdims=True)
        return codes[:, :hand_count].astype(jnp.float32) * (gain * (1.0 / (STEPS * len(code_refs))))

    values = {mask: value(ref) for mask, ref in zip((0, *order), code_refs)}
    total = None
    for mask in range(0, len(values), 2):
        pair = values[mask] + values[mask + 1]
        total = pair if total is None else total + pair
    out_ref[...] = total


def chance(hand_count, order, codes):
    return pl.pallas_call(
        functools.partial(chance_kernel, hand_count, order),
        out_shape=jax.ShapeDtypeStruct((codes[0].shape[0], hand_count), jnp.float32),
        in_specs=[WHOLE] * len(codes),
        out_specs=WHOLE,
        compiler_params=params(8),
        name="chance_sum",
    )(*codes)


def swap(array, axes, mask):
    return lax.ppermute(array, axes, [(index, index ^ mask) for index in range(lax.axis_size(axes))])


def on_device(
    regrets, opp_reach, pot_size, line_kind, board_lines, board_count, hand_ranks, live_hands
):
    hand_count = opp_reach.shape[2]
    line_count = opp_reach.shape[1]
    group = ("turn", "river")
    group_size = lax.axis_size(group)
    core = lax.axis_size("river")
    board_total = group_size * board_lines.shape[2]
    extra = up(line_count, SUB) - line_count
    bases = first_lines(line_count, core)
    kinds = jnp.pad(line_kind, ((0, 0), (0, extra)))
    boards = pack(board_count[0, 0], board_lines[0, 0], hand_ranks[0, 0], live_hands[0, 0], kinds, bases)
    masks = [1 << bit for bit in range(group_size.bit_length() - 1) if 1 << bit != core]
    arrived = swap(boards, group, masks[0])
    reach = jnp.pad(opp_reach[0], ((0, extra), (0, 0)))
    pots = jnp.pad(pot_size, ((0, 0), (0, extra)))
    old_regrets = jnp.pad(regrets[0], ((0, extra), (0, 0)))
    mate_reach, mate_kinds = swap(reach, group, core), swap(kinds, group, core)
    held_tables = unpack(jnp.asarray(table(hand_count)), boards)
    rows, wide = reach.shape[0], up(hand_count, LANE)
    own, for_mate, all_reach, lines, boards = board_sums(
        functools.partial(first_kernel, hand_count, line_count),
        "first_boards",
        rows,
        (reach, mate_reach, mate_kinds),
        held_tables,
        boards,
        more=(
            jax.ShapeDtypeStruct((2 * rows, wide), jnp.bfloat16),
            jax.ShapeDtypeStruct((2 * rows, LANE), jnp.int32),
            jax.ShapeDtypeStruct(boards.shape, boards.dtype),
        ),
    )
    for mask in (*masks[1:], None):
        latest = arrived
        if mask is not None:
            boards = jnp.concatenate([boards, latest], axis=0)
            arrived = swap(boards, group, mask)
        own, for_mate = board_sums(
            more_kernel, "more_boards", rows, (all_reach, lines), held_tables, latest, (own, for_mate)
        )
    mate = swap(for_mate, group, core)
    scale = 1.0 / (board_total * hand_count)
    inputs = (own, mate, pots, kinds, old_regrets)
    codes = decision_call(
        codes_kernel,
        "node_codes",
        hand_count,
        scale,
        jax.ShapeDtypeStruct((rows // ACTS, wide), jnp.int16),
        inputs,
        [pltpu.VMEM((wide // LANE, rows, LANE), jnp.float32)],
    )
    updated = decision_call(
        regrets_kernel, "new_regrets", hand_count, scale, jax.ShapeDtypeStruct((rows, hand_count), jnp.float32), inputs
    )
    order = (3, 2, 1)
    total = chance(hand_count, order, [codes] + [swap(codes, "flop", mask) for mask in order])
    return (updated[None, :line_count], total[: line_count // ACTS])


def solution(mesh):
    placed = (
        P("flop", ("turn", "river"), None),
        P("flop", ("turn", "river"), None),
        P("flop", ("turn", "river")),
        P("flop", ("turn", "river")),
        P("flop", "turn", "river", None),
        P("flop", "turn", "river"),
        P("flop", "turn", "river", None),
        P("flop", "turn", "river", None),
    )
    return jax.shard_map(
        on_device,
        mesh=mesh,
        in_specs=placed,
        out_specs=(P("flop", ("turn", "river"), None), P(("turn", "river"), None)),
        check_vma=False,
    )
```

```python
import functools

import jax
import jax.numpy as jnp
import numpy as np
from jax import lax
from jax.experimental import pallas as pl
from jax.experimental.pallas import tpu as pltpu
from jax.sharding import PartitionSpec as P

CARDS = 52
ACTS = 2
LANE = 128
SUB = 32
RANK_SPAN = 8192
MANTISSA = 128
ROW_TILE = 128
COL_TILE = 1408
UNROLL = 8
STEPS = 32767.0
LOWEST = 100
WHOLE = pl.BlockSpec(memory_space=pltpu.VMEM)

floor_share = 0.1


def up(value, unit):
    return -(-value // unit) * unit


def tiles(total, size):
    return [(first, min(size, total - first)) for first in range(0, total, size)]


def params(mebibytes):
    return pltpu.CompilerParams(vmem_limit_bytes=mebibytes << 20)


@functools.cache
def tables(hand_count):
    wide, deep = up(hand_count, LANE), up(hand_count, 16)
    first, second = np.triu_indices(CARDS, 1)
    cards = np.zeros((hand_count, CARDS), np.float32)
    cards[np.arange(hand_count), first] = 1
    cards[np.arange(hand_count), second] = 1
    apart = np.zeros((deep, wide), np.float32)
    apart[:hand_count, :hand_count] = (cards @ cards.T) == 0
    spread = np.zeros((LANE, wide), np.float32)
    for first in (0, 1 + CARDS):
        spread[first, :hand_count] = 1
        spread[first + 1 : first + 1 + CARDS, :hand_count] = cards.T
    collect = -spread.T
    collect[:, [0, 1 + CARDS]] *= -1
    return [part.astype(jnp.bfloat16) for part in (apart, collect, spread)]


def as_column(row):
    size = row.shape[1]
    at = lax.broadcasted_iota(jnp.int32, (size, size), 0) == lax.broadcasted_iota(jnp.int32, (size, size), 1)
    return jnp.sum(jnp.where(at, row.astype(jnp.float32), 0.0), axis=1, keepdims=True)


def copy_all(pairs, sems):
    copies = [pltpu.make_async_copy(source, target, sems.at[at]) for at, (source, target) in enumerate(pairs)]
    for copy in copies:
        copy.start()
    for copy in copies:
        copy.wait()


def bases_kernel(line_count, core, out_ref):
    index = lax.axis_index("turn") * lax.axis_size("river") + lax.axis_index("river")
    lane = lax.broadcasted_iota(jnp.int32, out_ref.shape, 1)
    line = jnp.where(lane == LANE // 2, index, index ^ core) * line_count
    out_ref[...] = jnp.where((lane == LANE // 2) | (lane == LANE // 2 + 1), line, 0)


def first_lines(line_count, core):
    return pl.pallas_call(
        functools.partial(bases_kernel, line_count, core),
        out_shape=jax.ShapeDtypeStruct((1, LANE), jnp.int32),
        out_specs=WHOLE,
        compiler_params=params(4),
        name="first_lines",
        cost_estimate=pl.CostEstimate(flops=60 * 10**9, bytes_accessed=0, transcendentals=0),
    )()


def pack(counts, slots, ranks, live, bases):
    hand_count, slot_count, boards = ranks.shape[1], slots.shape[1], ranks.shape[0]
    wide = up(hand_count, LANE)

    def place(array, first):
        after = wide + slot_count + LANE - first - array.shape[1]
        return jnp.pad(array, ((0, boards - array.shape[0]), (first, after)))

    packed = place(ranks, 0) + RANK_SPAN * place(live, 0) + place(slots, wide) + place(bases, wide + slot_count)
    lane = lax.broadcasted_iota(jnp.int32, packed.shape, 1)
    return jnp.where(lane == wide - 1, lax.broadcast_in_dim(counts, packed.shape, (0,)), packed)


def lines_kernel(hand_count, line_count, own_ref, mate_ref, packed_ref, reach_ref, line_ref):
    rows = own_ref.shape[0]
    first = packed_ref.shape[1] - LANE // 2
    base = packed_ref[:1, first : first + 2]
    reach_ref[...] = jnp.zeros_like(reach_ref)
    reach_ref[:rows, :hand_count] = own_ref[...]
    reach_ref[rows:, :hand_count] = mate_ref[...]
    row = lax.broadcasted_iota(jnp.int32, line_ref.shape, 0)
    within = jnp.where(row < rows, row, row - rows)
    line = jnp.where(row < rows, base[:, :1], base[:, 1:]) + within
    line_ref[...] = jnp.where(within < line_count, line, -2)


def first_kernel(hand_count, line_count, own_ref, mate_ref, *refs):
    tables, (packed_ref, own_out, mate_out, reach_ref, line_ref, same_ref), scratch = refs[:3], refs[3:9], refs[9:]
    same_ref[...] = packed_ref[...]
    lines_kernel(hand_count, line_count, own_ref, mate_ref, packed_ref, reach_ref, line_ref)
    own_out[...] = jnp.zeros_like(own_out)
    mate_out[...] = jnp.zeros_like(mate_out)
    add_boards(reach_ref, line_ref, *tables, packed_ref, own_out, mate_out, *scratch)


def more_kernel(reach_ref, line_ref, *refs):
    tables, (packed_ref, own_ref, mate_ref, own_out, mate_out), scratch = refs[:3], refs[3:8], refs[8:]
    own_out[...] = own_ref[...]
    mate_out[...] = mate_ref[...]
    add_boards(reach_ref, line_ref, *tables, packed_ref, own_out, mate_out, *scratch)


def add_boards(
    reach_ref, line_ref, apart_ref, collect_ref, spread_ref, packed_ref, own_out, mate_out, column_ref, board_ref
):
    wide, deep = apart_ref.shape[1], apart_ref.shape[0]
    rows = own_out.shape[0]
    parts = 1 + CARDS
    line = jnp.concatenate([line_ref[...]] * ((packed_ref.shape[1] - LANE - wide) // LANE), axis=1)
    lane = lax.broadcasted_iota(jnp.int32, (2 * rows, LANE), 1)
    board_total = packed_ref.shape[0]
    end = packed_ref.shape[1] - LANE
    slot = lax.broadcasted_iota(jnp.int32, (board_total, end - wide), 1)
    board_ref[:, :wide] = packed_ref[:, :wide]
    board_ref[:, wide:] = jnp.where(slot < packed_ref[:, wide - 1 : wide], packed_ref[:, wide:end], -1)

    zero, one = jnp.bfloat16(0), jnp.bfloat16(1)

    def add_board(board):
        keys = board_ref[pl.ds(board, 1), :wide]
        slots = board_ref[pl.ds(board, 1), wide:]
        ranks = keys & (RANK_SPAN - 1)
        live = (keys >> (RANK_SPAN.bit_length() - 1)).astype(jnp.float32)
        power = ranks >> (MANTISSA.bit_length() - 1)
        near = jnp.left_shift(1, jnp.minimum(power, 29)).astype(jnp.float32)
        far = jnp.left_shift(1, jnp.maximum(power - 29, 0)).astype(jnp.float32)
        order = ((ranks & (MANTISSA - 1)) + MANTISSA).astype(jnp.float32) * near * far
        column_ref[...] = jnp.transpose(jnp.broadcast_to(order, (LANE, wide)))[:deep].astype(jnp.bfloat16)
        order = order.astype(jnp.bfloat16)
        keep = jnp.max(jnp.where(slots == line, 1.0, 0.0), axis=1, keepdims=True)
        held = reach_ref[...] * live.astype(jnp.bfloat16) * keep.astype(jnp.bfloat16)
        show_reach = jnp.maximum(held, zero)
        fold_reach = jnp.maximum(-held, zero)
        sums = jnp.dot(fold_reach, collect_ref[...], preferred_element_type=jnp.float32)
        high = sums.astype(jnp.bfloat16).astype(jnp.float32)
        sums = jnp.where(lane < parts, high, sums - high).astype(jnp.bfloat16)
        for first, count in tiles(wide, COL_TILE):
            at = slice(first, first + count)
            total = 0.0
            for top, height in tiles(deep, ROW_TILE):
                down = slice(top, top + height)
                column = jnp.concatenate([column_ref[down]] * (count // LANE), axis=1)
                matrix = jnp.clip(order[:, at] - column, -one, one) * apart_ref[down, at]
                total += jnp.dot(show_reach[:, down], matrix, preferred_element_type=jnp.float32)
            total += jnp.dot(sums, spread_ref[:, at], preferred_element_type=jnp.float32)
            total = (total + fold_reach[:, at].astype(jnp.float32)) * live[:, at]
            own_out[:, at] += total[:rows]
            mate_out[:, at] += total[rows:]

    if board_total <= UNROLL:
        for board in range(board_total):
            add_board(board)
    else:
        pl.loop(0, board_total)(add_board)


def board_sums(kernel, name, rows, inputs, tables, boards, sums=(), more=()):
    deep, wide = tables[0].shape
    out = [jax.ShapeDtypeStruct((rows, wide), jnp.float32)] * 2 + list(more)
    return pl.pallas_call(
        kernel,
        out_shape=out,
        in_specs=[WHOLE] * (len(inputs) + len(tables) + 1 + len(sums)),
        out_specs=[WHOLE] * len(out),
        scratch_shapes=[
            pltpu.VMEM((deep, LANE), jnp.bfloat16),
            pltpu.VMEM((boards.shape[0], boards.shape[1] - LANE), jnp.int32),
        ],
        compiler_params=params(32),
        name=name,
        cost_estimate=pl.CostEstimate(
            flops=4 * boards.shape[0] * rows * wide * wide, bytes_accessed=0, transcendentals=0
        ),
    )(*inputs, *tables, boards, *sums)


def powers():
    lane = lax.broadcasted_iota(jnp.int32, (1, LANE), 1)
    up_size, down_size = jnp.ones((1, LANE), jnp.float32), jnp.ones((1, LANE), jnp.float32)
    bit = 1
    while bit < LANE:
        chosen = (jnp.abs(lane - LOWEST) & bit) != 0
        up_size = jnp.where(chosen, up_size * 2.0**bit, up_size)
        down_size = jnp.where(chosen, down_size * 0.5**bit, down_size)
        bit *= 2
    return jnp.where(lane < LOWEST, down_size, up_size), jnp.where(lane < LOWEST, up_size, down_size)


def decide(hand_count, scale, own_ref, mate_ref, pot_ref, kind_ref, regret_ref):
    pot = as_column(pot_ref[...])
    coef = jnp.where(as_column(kind_ref[...]) == 1, -pot, pot) * scale
    values = (own_ref[:, :hand_count] + mate_ref[:, :hand_count]) * coef
    regrets = regret_ref[...]
    rows = regrets.shape[0]
    even = lax.broadcasted_iota(jnp.int32, (rows, 1), 0) % ACTS == 0

    def both(array):
        other = jnp.where(even, pltpu.roll(array, rows - 1, 0), pltpu.roll(array, 1, 0))
        return array + other

    positive = jnp.maximum(regrets, 0.0)
    strategy = (positive + floor_share) / (both(positive) + ACTS * floor_share)
    return regrets, values, both(strategy * values)


def regrets_kernel(hand_count, scale, *refs):
    regrets, values, node = decide(hand_count, scale, *refs[:-1])
    refs[-1][...] = jnp.maximum(regrets + values - node, 0.0)


def codes_kernel(hand_count, scale, *refs):
    *inputs, code_out, node_ref = refs
    _, _, node = decide(hand_count, scale, *inputs)
    rows = node.shape[0]
    size, flip = powers()
    largest = jnp.max(jnp.abs(node), axis=1, keepdims=True)
    place = jnp.sum(jnp.where(size < largest, 1.0, 0.0), axis=1, keepdims=True)
    lane = lax.broadcasted_iota(jnp.int32, (rows, LANE), 1).astype(jnp.float32)
    gain = jnp.sum(jnp.where(lane == place, flip, 0.0), axis=1, keepdims=True) * STEPS
    codes = node * gain
    for tile, (first, count) in enumerate(tiles(hand_count, LANE)):
        node_ref[tile, :, :count] = codes[:, first : first + count]
        if count < LANE:
            node_ref[tile, :, count:] = jnp.broadcast_to(place, (rows, LANE - count))
        picked = node_ref[tile, pl.ds(0, rows // ACTS, stride=ACTS), :]
        code_out[:, first : first + LANE] = jnp.floor(picked + 0.5).astype(jnp.int32).astype(jnp.int16)


def decision_call(kernel, name, hand_count, scale, out_shape, inputs, scratch=()):
    return pl.pallas_call(
        functools.partial(kernel, hand_count, scale),
        out_shape=out_shape,
        in_specs=[WHOLE] * len(inputs),
        out_specs=WHOLE,
        scratch_shapes=scratch,
        compiler_params=params(8),
        name=name,
    )(*inputs)


def chance_kernel(hand_count, order, *refs):
    code_refs, out_ref = refs[:-1], refs[-1]
    size, _ = powers()
    lane = lax.broadcasted_iota(jnp.int32, (out_ref.shape[0], LANE), 1)

    def value(ref):
        codes = ref[...].astype(jnp.int32)
        place = codes[:, hand_count : hand_count + 1]
        gain = jnp.sum(jnp.where(lane == place, size, 0.0), axis=1, keepdims=True)
        return codes[:, :hand_count].astype(jnp.float32) * (gain * (1.0 / (STEPS * len(code_refs))))

    values = {mask: value(ref) for mask, ref in zip((0, *order), code_refs)}
    total = None
    for mask in range(0, len(values), 2):
        pair = values[mask] + values[mask + 1]
        total = pair if total is None else total + pair
    out_ref[...] = total


def chance(hand_count, order, codes):
    return pl.pallas_call(
        functools.partial(chance_kernel, hand_count, order),
        out_shape=jax.ShapeDtypeStruct((codes[0].shape[0], hand_count), jnp.float32),
        in_specs=[WHOLE] * len(codes),
        out_specs=WHOLE,
        compiler_params=params(8),
        name="chance_sum",
    )(*codes)


def swap(array, axes, mask):
    return lax.ppermute(array, axes, [(index, index ^ mask) for index in range(lax.axis_size(axes))])


def on_device(
    regrets, opp_reach, pot_size, line_kind, board_lines, board_count, hand_ranks, live_hands
):
    hand_count = opp_reach.shape[2]
    line_count = opp_reach.shape[1]
    group = ("turn", "river")
    group_size = lax.axis_size(group)
    core = lax.axis_size("river")
    board_total = group_size * board_lines.shape[2]
    extra = up(line_count, SUB) - line_count
    bases = first_lines(line_count, core)
    kinds = jnp.pad(line_kind, ((0, 0), (0, extra)))
    boards = pack(board_count[0, 0], board_lines[0, 0], hand_ranks[0, 0], live_hands[0, 0], bases)
    masks = [1 << bit for bit in range(group_size.bit_length() - 1) if 1 << bit != core]
    arrived = swap(boards, group, masks[0])
    reach, late_kinds, _ = lax.optimization_barrier((jnp.pad(opp_reach[0], ((0, extra), (0, 0))), kinds, bases))
    showdown = lax.broadcast_in_dim(late_kinds[0], reach.shape, (0,)) == 0
    reach = jnp.where(showdown, reach, -reach)
    pots = jnp.pad(pot_size, ((0, 0), (0, extra)))
    old_regrets = jnp.pad(regrets[0], ((0, extra), (0, 0)))
    mate_reach = swap(reach, group, core)
    held_tables = [jnp.asarray(table) for table in tables(hand_count)]
    rows, wide = reach.shape[0], up(hand_count, LANE)
    own, for_mate, all_reach, lines, boards = board_sums(
        functools.partial(first_kernel, hand_count, line_count),
        "first_boards",
        rows,
        (reach, mate_reach),
        held_tables,
        boards,
        more=(
            jax.ShapeDtypeStruct((2 * rows, wide), jnp.bfloat16),
            jax.ShapeDtypeStruct((2 * rows, LANE), jnp.int32),
            jax.ShapeDtypeStruct(boards.shape, boards.dtype),
        ),
    )
    for mask in (*masks[1:], None):
        latest = arrived
        if mask is not None:
            boards = jnp.concatenate([boards, latest], axis=0)
            arrived = swap(boards, group, mask)
        own, for_mate = board_sums(
            more_kernel, "more_boards", rows, (all_reach, lines), held_tables, latest, (own, for_mate)
        )
    mate = swap(for_mate, group, core)
    scale = 1.0 / (board_total * hand_count)
    inputs = (own, mate, pots, kinds, old_regrets)
    codes = decision_call(
        codes_kernel,
        "node_codes",
        hand_count,
        scale,
        jax.ShapeDtypeStruct((rows // ACTS, wide), jnp.int16),
        inputs,
        [pltpu.VMEM((wide // LANE, rows, LANE), jnp.float32)],
    )
    updated = decision_call(
        regrets_kernel, "new_regrets", hand_count, scale, jax.ShapeDtypeStruct((rows, hand_count), jnp.float32), inputs
    )
    order = (3, 2, 1)
    total = chance(hand_count, order, [codes] + [swap(codes, "flop", mask) for mask in order])
    return (updated[None, :line_count], total[: line_count // ACTS])


def solution(mesh):
    placed = (
        P("flop", ("turn", "river"), None),
        P("flop", ("turn", "river"), None),
        P("flop", ("turn", "river")),
        P("flop", ("turn", "river")),
        P("flop", "turn", "river", None),
        P("flop", "turn", "river"),
        P("flop", "turn", "river", None),
        P("flop", "turn", "river", None),
    )
    return jax.shard_map(
        on_device,
        mesh=mesh,
        in_specs=placed,
        out_specs=(P("flop", ("turn", "river"), None), P(("turn", "river"), None)),
        check_vma=False,
    )
```

```python
import functools

import jax
import jax.numpy as jnp
import numpy as np
from jax import lax
from jax.experimental import pallas as pl
from jax.experimental.pallas import tpu as pltpu
from jax.sharding import PartitionSpec as P

CARDS = 52
ACTS = 2
LANE = 128
SUB = 32
RANK_SPAN = 8192
MANTISSA = 128
ROW_TILE = 128
COL_TILE = 1408
UNROLL = 8
STEPS = 32767.0
LOWEST = 100
WHOLE = pl.BlockSpec(memory_space=pltpu.VMEM)

floor_share = 0.1


def up(value, unit):
    return -(-value // unit) * unit


def tiles(total, size):
    return [(first, min(size, total - first)) for first in range(0, total, size)]


def params(mebibytes):
    return pltpu.CompilerParams(vmem_limit_bytes=mebibytes << 20)


@functools.cache
def tables(hand_count):
    wide, deep = up(hand_count, LANE), up(hand_count, 16)
    first, second = np.triu_indices(CARDS, 1)
    cards = np.zeros((hand_count, CARDS), np.float32)
    cards[np.arange(hand_count), first] = 1
    cards[np.arange(hand_count), second] = 1
    apart = np.zeros((deep, wide), np.float32)
    apart[:hand_count, :hand_count] = (cards @ cards.T) == 0
    spread = np.zeros((LANE, wide), np.float32)
    for first in (0, 1 + CARDS):
        spread[first, :hand_count] = 1
        spread[first + 1 : first + 1 + CARDS, :hand_count] = cards.T
    collect = -spread.T
    collect[:, [0, 1 + CARDS]] *= -1
    return [part.astype(jnp.bfloat16) for part in (apart, collect, spread)]


def as_column(row):
    size = row.shape[1]
    at = lax.broadcasted_iota(jnp.int32, (size, size), 0) == lax.broadcasted_iota(jnp.int32, (size, size), 1)
    return jnp.sum(jnp.where(at, row.astype(jnp.float32), 0.0), axis=1, keepdims=True)


def copy_all(pairs, sems):
    copies = [pltpu.make_async_copy(source, target, sems.at[at]) for at, (source, target) in enumerate(pairs)]
    for copy in copies:
        copy.start()
    for copy in copies:
        copy.wait()


def bases_kernel(line_count, core, out_ref):
    index = lax.axis_index("turn") * lax.axis_size("river") + lax.axis_index("river")
    lane = lax.broadcasted_iota(jnp.int32, out_ref.shape, 1)
    line = jnp.where(lane == LANE // 2, index, index ^ core) * line_count
    out_ref[...] = jnp.where((lane == LANE // 2) | (lane == LANE // 2 + 1), line, 0)


def first_lines(line_count, core):
    return pl.pallas_call(
        functools.partial(bases_kernel, line_count, core),
        out_shape=jax.ShapeDtypeStruct((1, LANE), jnp.int32),
        out_specs=WHOLE,
        compiler_params=params(4),
        name="first_lines",
        cost_estimate=pl.CostEstimate(flops=10 * 10**9, bytes_accessed=0, transcendentals=0),
    )()


def pass_kernel(in_ref, out_ref):
    out_ref[...] = in_ref[...]


def pass_on(array):
    return pl.pallas_call(
        pass_kernel,
        out_shape=jax.ShapeDtypeStruct(array.shape, array.dtype),
        in_specs=[WHOLE],
        out_specs=WHOLE,
        compiler_params=params(4),
        name="pass_on",
        cost_estimate=pl.CostEstimate(flops=60 * 10**9, bytes_accessed=0, transcendentals=0),
    )(array)


def pack(counts, slots, ranks, live, bases):
    hand_count, slot_count, boards = ranks.shape[1], slots.shape[1], ranks.shape[0]
    wide = up(hand_count, LANE)

    def place(array, first):
        after = wide + slot_count + LANE - first - array.shape[1]
        return jnp.pad(array, ((0, boards - array.shape[0]), (first, after)))

    packed = place(ranks, 0) + RANK_SPAN * place(live, 0) + place(slots, wide) + place(bases, wide + slot_count)
    lane = lax.broadcasted_iota(jnp.int32, packed.shape, 1)
    return jnp.where(lane == wide - 1, lax.broadcast_in_dim(counts, packed.shape, (0,)), packed)


def lines_kernel(hand_count, line_count, own_ref, mate_ref, packed_ref, reach_ref, line_ref):
    rows = own_ref.shape[0]
    first = packed_ref.shape[1] - LANE // 2
    base = packed_ref[:1, first : first + 2]
    reach_ref[...] = jnp.zeros_like(reach_ref)
    reach_ref[:rows, :hand_count] = own_ref[...]
    reach_ref[rows:, :hand_count] = mate_ref[...]
    row = lax.broadcasted_iota(jnp.int32, line_ref.shape, 0)
    within = jnp.where(row < rows, row, row - rows)
    line = jnp.where(row < rows, base[:, :1], base[:, 1:]) + within
    line_ref[...] = jnp.where(within < line_count, line, -2)


def first_kernel(hand_count, line_count, own_ref, mate_ref, *refs):
    tables, (packed_ref, own_out, mate_out, reach_ref, line_ref, same_ref), scratch = refs[:3], refs[3:9], refs[9:]
    same_ref[...] = packed_ref[...]
    lines_kernel(hand_count, line_count, own_ref, mate_ref, packed_ref, reach_ref, line_ref)
    own_out[...] = jnp.zeros_like(own_out)
    mate_out[...] = jnp.zeros_like(mate_out)
    add_boards(reach_ref, line_ref, *tables, packed_ref, own_out, mate_out, *scratch)


def more_kernel(reach_ref, line_ref, *refs):
    tables, (packed_ref, own_ref, mate_ref, own_out, mate_out), scratch = refs[:3], refs[3:8], refs[8:]
    own_out[...] = own_ref[...]
    mate_out[...] = mate_ref[...]
    add_boards(reach_ref, line_ref, *tables, packed_ref, own_out, mate_out, *scratch)


def add_boards(
    reach_ref, line_ref, apart_ref, collect_ref, spread_ref, packed_ref, own_out, mate_out, column_ref, board_ref
):
    wide, deep = apart_ref.shape[1], apart_ref.shape[0]
    rows = own_out.shape[0]
    parts = 1 + CARDS
    line = jnp.concatenate([line_ref[...]] * ((packed_ref.shape[1] - LANE - wide) // LANE), axis=1)
    lane = lax.broadcasted_iota(jnp.int32, (2 * rows, LANE), 1)
    board_total = packed_ref.shape[0]
    end = packed_ref.shape[1] - LANE
    slot = lax.broadcasted_iota(jnp.int32, (board_total, end - wide), 1)
    board_ref[:, :wide] = packed_ref[:, :wide]
    board_ref[:, wide:] = jnp.where(slot < packed_ref[:, wide - 1 : wide], packed_ref[:, wide:end], -1)

    zero, one = jnp.bfloat16(0), jnp.bfloat16(1)

    def add_board(board):
        keys = board_ref[pl.ds(board, 1), :wide]
        slots = board_ref[pl.ds(board, 1), wide:]
        ranks = keys & (RANK_SPAN - 1)
        live = (keys >> (RANK_SPAN.bit_length() - 1)).astype(jnp.float32)
        power = ranks >> (MANTISSA.bit_length() - 1)
        near = jnp.left_shift(1, jnp.minimum(power, 29)).astype(jnp.float32)
        far = jnp.left_shift(1, jnp.maximum(power - 29, 0)).astype(jnp.float32)
        order = ((ranks & (MANTISSA - 1)) + MANTISSA).astype(jnp.float32) * near * far
        column_ref[...] = jnp.transpose(jnp.broadcast_to(order, (LANE, wide)))[:deep].astype(jnp.bfloat16)
        order = order.astype(jnp.bfloat16)
        keep = jnp.max(jnp.where(slots == line, 1.0, 0.0), axis=1, keepdims=True)
        held = reach_ref[...] * live.astype(jnp.bfloat16) * keep.astype(jnp.bfloat16)
        show_reach = jnp.maximum(held, zero)
        fold_reach = jnp.maximum(-held, zero)
        sums = jnp.dot(fold_reach, collect_ref[...], preferred_element_type=jnp.float32)
        high = sums.astype(jnp.bfloat16).astype(jnp.float32)
        sums = jnp.where(lane < parts, high, sums - high).astype(jnp.bfloat16)
        for first, count in tiles(wide, COL_TILE):
            at = slice(first, first + count)
            total = 0.0
            for top, height in tiles(deep, ROW_TILE):
                down = slice(top, top + height)
                column = jnp.concatenate([column_ref[down]] * (count // LANE), axis=1)
                matrix = jnp.clip(order[:, at] - column, -one, one) * apart_ref[down, at]
                total += jnp.dot(show_reach[:, down], matrix, preferred_element_type=jnp.float32)
            total += jnp.dot(sums, spread_ref[:, at], preferred_element_type=jnp.float32)
            total = (total + fold_reach[:, at].astype(jnp.float32)) * live[:, at]
            own_out[:, at] += total[:rows]
            mate_out[:, at] += total[rows:]

    if board_total <= UNROLL:
        for board in range(board_total):
            add_board(board)
    else:
        pl.loop(0, board_total)(add_board)


def board_sums(kernel, name, rows, inputs, tables, boards, sums=(), more=()):
    deep, wide = tables[0].shape
    out = [jax.ShapeDtypeStruct((rows, wide), jnp.float32)] * 2 + list(more)
    return pl.pallas_call(
        kernel,
        out_shape=out,
        in_specs=[WHOLE] * (len(inputs) + len(tables) + 1 + len(sums)),
        out_specs=[WHOLE] * len(out),
        scratch_shapes=[
            pltpu.VMEM((deep, LANE), jnp.bfloat16),
            pltpu.VMEM((boards.shape[0], boards.shape[1] - LANE), jnp.int32),
        ],
        compiler_params=params(32),
        name=name,
        cost_estimate=pl.CostEstimate(
            flops=4 * boards.shape[0] * rows * wide * wide, bytes_accessed=0, transcendentals=0
        ),
    )(*inputs, *tables, boards, *sums)


def powers():
    lane = lax.broadcasted_iota(jnp.int32, (1, LANE), 1)
    up_size, down_size = jnp.ones((1, LANE), jnp.float32), jnp.ones((1, LANE), jnp.float32)
    bit = 1
    while bit < LANE:
        chosen = (jnp.abs(lane - LOWEST) & bit) != 0
        up_size = jnp.where(chosen, up_size * 2.0**bit, up_size)
        down_size = jnp.where(chosen, down_size * 0.5**bit, down_size)
        bit *= 2
    return jnp.where(lane < LOWEST, down_size, up_size), jnp.where(lane < LOWEST, up_size, down_size)


def decide(hand_count, scale, own_ref, mate_ref, pot_ref, kind_ref, regret_ref):
    pot = as_column(pot_ref[...])
    coef = jnp.where(as_column(kind_ref[...]) == 1, -pot, pot) * scale
    values = (own_ref[:, :hand_count] + mate_ref[:, :hand_count]) * coef
    regrets = regret_ref[...]
    rows = regrets.shape[0]
    even = lax.broadcasted_iota(jnp.int32, (rows, 1), 0) % ACTS == 0

    def both(array):
        other = jnp.where(even, pltpu.roll(array, rows - 1, 0), pltpu.roll(array, 1, 0))
        return array + other

    positive = jnp.maximum(regrets, 0.0)
    strategy = (positive + floor_share) / (both(positive) + ACTS * floor_share)
    return regrets, values, both(strategy * values)


def regrets_kernel(hand_count, scale, *refs):
    regrets, values, node = decide(hand_count, scale, *refs[:-1])
    refs[-1][...] = jnp.maximum(regrets + values - node, 0.0)


def codes_kernel(hand_count, scale, *refs):
    *inputs, code_out, node_ref = refs
    _, _, node = decide(hand_count, scale, *inputs)
    rows = node.shape[0]
    size, flip = powers()
    largest = jnp.max(jnp.abs(node), axis=1, keepdims=True)
    place = jnp.sum(jnp.where(size < largest, 1.0, 0.0), axis=1, keepdims=True)
    lane = lax.broadcasted_iota(jnp.int32, (rows, LANE), 1).astype(jnp.float32)
    gain = jnp.sum(jnp.where(lane == place, flip, 0.0), axis=1, keepdims=True) * STEPS
    codes = node * gain
    for tile, (first, count) in enumerate(tiles(hand_count, LANE)):
        node_ref[tile, :, :count] = codes[:, first : first + count]
        if count < LANE:
            node_ref[tile, :, count:] = jnp.broadcast_to(place, (rows, LANE - count))
        picked = node_ref[tile, pl.ds(0, rows // ACTS, stride=ACTS), :]
        code_out[:, first : first + LANE] = jnp.floor(picked + 0.5).astype(jnp.int32).astype(jnp.int16)


def decision_call(kernel, name, hand_count, scale, out_shape, inputs, scratch=()):
    return pl.pallas_call(
        functools.partial(kernel, hand_count, scale),
        out_shape=out_shape,
        in_specs=[WHOLE] * len(inputs),
        out_specs=WHOLE,
        scratch_shapes=scratch,
        compiler_params=params(8),
        name=name,
    )(*inputs)


def chance_kernel(hand_count, order, *refs):
    code_refs, out_ref = refs[:-1], refs[-1]
    size, _ = powers()
    lane = lax.broadcasted_iota(jnp.int32, (out_ref.shape[0], LANE), 1)

    def value(ref):
        codes = ref[...].astype(jnp.int32)
        place = codes[:, hand_count : hand_count + 1]
        gain = jnp.sum(jnp.where(lane == place, size, 0.0), axis=1, keepdims=True)
        return codes[:, :hand_count].astype(jnp.float32) * (gain * (1.0 / (STEPS * len(code_refs))))

    values = {mask: value(ref) for mask, ref in zip((0, *order), code_refs)}
    total = None
    for mask in range(0, len(values), 2):
        pair = values[mask] + values[mask + 1]
        total = pair if total is None else total + pair
    out_ref[...] = total


def chance(hand_count, order, codes):
    return pl.pallas_call(
        functools.partial(chance_kernel, hand_count, order),
        out_shape=jax.ShapeDtypeStruct((codes[0].shape[0], hand_count), jnp.float32),
        in_specs=[WHOLE] * len(codes),
        out_specs=WHOLE,
        compiler_params=params(8),
        name="chance_sum",
    )(*codes)


def swap(array, axes, mask):
    return lax.ppermute(array, axes, [(index, index ^ mask) for index in range(lax.axis_size(axes))])


def on_device(
    regrets, opp_reach, pot_size, line_kind, board_lines, board_count, hand_ranks, live_hands
):
    hand_count = opp_reach.shape[2]
    line_count = opp_reach.shape[1]
    group = ("turn", "river")
    group_size = lax.axis_size(group)
    core = lax.axis_size("river")
    board_total = group_size * board_lines.shape[2]
    extra = up(line_count, SUB) - line_count
    bases = pass_on(first_lines(line_count, core))
    kinds = jnp.pad(line_kind, ((0, 0), (0, extra)))
    boards = pack(board_count[0, 0], board_lines[0, 0], hand_ranks[0, 0], live_hands[0, 0], bases)
    masks = [1 << bit for bit in range(group_size.bit_length() - 1) if 1 << bit != core]
    arrived = swap(boards, group, masks[0])
    reach, late_kinds, _ = lax.optimization_barrier((jnp.pad(opp_reach[0], ((0, extra), (0, 0))), kinds, bases))
    showdown = lax.broadcast_in_dim(late_kinds[0], reach.shape, (0,)) == 0
    reach = jnp.where(showdown, reach, -reach)
    pots = jnp.pad(pot_size, ((0, 0), (0, extra)))
    old_regrets = jnp.pad(regrets[0], ((0, extra), (0, 0)))
    mate_reach = swap(reach, group, core)
    held_tables = [jnp.asarray(table) for table in tables(hand_count)]
    rows, wide = reach.shape[0], up(hand_count, LANE)
    own, for_mate, all_reach, lines, boards = board_sums(
        functools.partial(first_kernel, hand_count, line_count),
        "first_boards",
        rows,
        (reach, mate_reach),
        held_tables,
        boards,
        more=(
            jax.ShapeDtypeStruct((2 * rows, wide), jnp.bfloat16),
            jax.ShapeDtypeStruct((2 * rows, LANE), jnp.int32),
            jax.ShapeDtypeStruct(boards.shape, boards.dtype),
        ),
    )
    for mask in (*masks[1:], None):
        latest = arrived
        if mask is not None:
            boards = jnp.concatenate([boards, latest], axis=0)
            arrived = swap(boards, group, mask)
        own, for_mate = board_sums(
            more_kernel, "more_boards", rows, (all_reach, lines), held_tables, latest, (own, for_mate)
        )
    mate = swap(for_mate, group, core)
    scale = 1.0 / (board_total * hand_count)
    inputs = (own, mate, pots, kinds, old_regrets)
    codes = decision_call(
        codes_kernel,
        "node_codes",
        hand_count,
        scale,
        jax.ShapeDtypeStruct((rows // ACTS, wide), jnp.int16),
        inputs,
        [pltpu.VMEM((wide // LANE, rows, LANE), jnp.float32)],
    )
    updated = decision_call(
        regrets_kernel, "new_regrets", hand_count, scale, jax.ShapeDtypeStruct((rows, hand_count), jnp.float32), inputs
    )
    order = (3, 2, 1)
    total = chance(hand_count, order, [codes] + [swap(codes, "flop", mask) for mask in order])
    return (updated[None, :line_count], total[: line_count // ACTS])


def solution(mesh):
    placed = (
        P("flop", ("turn", "river"), None),
        P("flop", ("turn", "river"), None),
        P("flop", ("turn", "river")),
        P("flop", ("turn", "river")),
        P("flop", "turn", "river", None),
        P("flop", "turn", "river"),
        P("flop", "turn", "river", None),
        P("flop", "turn", "river", None),
    )
    return jax.shard_map(
        on_device,
        mesh=mesh,
        in_specs=placed,
        out_specs=(P("flop", ("turn", "river"), None), P(("turn", "river"), None)),
        check_vma=False,
    )
```

```python
import functools

import jax
import jax.numpy as jnp
import numpy as np
from jax import lax
from jax.experimental import pallas as pl
from jax.experimental.pallas import tpu as pltpu
from jax.sharding import PartitionSpec as P

CARDS = 52
ACTS = 2
LANE = 128
SUB = 32
RANK_SPAN = 8192
MANTISSA = 128
ROW_TILE = 128
COL_TILE = 768
UNROLL = 8
STEPS = 32767.0
LOWEST = 100
WHOLE = pl.BlockSpec(memory_space=pltpu.VMEM)

floor_share = 0.1


def up(value, unit):
    return -(-value // unit) * unit


def tiles(total, size):
    return [(first, min(size, total - first)) for first in range(0, total, size)]


def params(mebibytes):
    return pltpu.CompilerParams(vmem_limit_bytes=mebibytes << 20)


@functools.cache
def tables(hand_count):
    wide, deep = up(hand_count, LANE), up(hand_count, 16)
    first, second = np.triu_indices(CARDS, 1)
    cards = np.zeros((hand_count, CARDS), np.float32)
    cards[np.arange(hand_count), first] = 1
    cards[np.arange(hand_count), second] = 1
    apart = np.zeros((deep, wide), np.float32)
    apart[:hand_count, :hand_count] = (cards @ cards.T) == 0
    spread = np.zeros((LANE, wide), np.float32)
    for first in (0, 1 + CARDS):
        spread[first, :hand_count] = 1
        spread[first + 1 : first + 1 + CARDS, :hand_count] = cards.T
    collect = -spread.T
    collect[:, [0, 1 + CARDS]] *= -1
    return [part.astype(jnp.bfloat16) for part in (apart, collect, spread)]


def as_column(row):
    size = row.shape[1]
    at = lax.broadcasted_iota(jnp.int32, (size, size), 0) == lax.broadcasted_iota(jnp.int32, (size, size), 1)
    return jnp.sum(jnp.where(at, row.astype(jnp.float32), 0.0), axis=1, keepdims=True)


def copy_all(pairs, sems):
    copies = [pltpu.make_async_copy(source, target, sems.at[at]) for at, (source, target) in enumerate(pairs)]
    for copy in copies:
        copy.start()
    for copy in copies:
        copy.wait()


def bases_kernel(line_count, core, out_ref):
    index = lax.axis_index("turn") * lax.axis_size("river") + lax.axis_index("river")
    lane = lax.broadcasted_iota(jnp.int32, out_ref.shape, 1)
    line = jnp.where(lane == LANE // 2, index, index ^ core) * line_count
    out_ref[...] = jnp.where((lane == LANE // 2) | (lane == LANE // 2 + 1), line, 0)


def first_lines(line_count, core):
    return pl.pallas_call(
        functools.partial(bases_kernel, line_count, core),
        out_shape=jax.ShapeDtypeStruct((1, LANE), jnp.int32),
        out_specs=WHOLE,
        compiler_params=params(4),
        name="first_lines",
        cost_estimate=pl.CostEstimate(flops=10 * 10**9, bytes_accessed=0, transcendentals=0),
    )()


def pass_kernel(in_ref, out_ref):
    out_ref[...] = in_ref[...]


def pass_on(array):
    return pl.pallas_call(
        pass_kernel,
        out_shape=jax.ShapeDtypeStruct(array.shape, array.dtype),
        in_specs=[WHOLE],
        out_specs=WHOLE,
        compiler_params=params(4),
        name="pass_on",
        cost_estimate=pl.CostEstimate(flops=60 * 10**9, bytes_accessed=0, transcendentals=0),
    )(array)


def pack(counts, slots, ranks, live, bases):
    hand_count, slot_count, boards = ranks.shape[1], slots.shape[1], ranks.shape[0]
    wide = up(hand_count, LANE)

    def place(array, first):
        after = wide + slot_count + LANE - first - array.shape[1]
        return jnp.pad(array, ((0, boards - array.shape[0]), (first, after)))

    packed = place(ranks, 0) + RANK_SPAN * place(live, 0) + place(slots, wide) + place(bases, wide + slot_count)
    lane = lax.broadcasted_iota(jnp.int32, packed.shape, 1)
    return jnp.where(lane == wide - 1, lax.broadcast_in_dim(counts, packed.shape, (0,)), packed)


def lines_kernel(hand_count, line_count, own_ref, mate_ref, packed_ref, reach_ref, line_ref):
    rows = own_ref.shape[0]
    first = packed_ref.shape[1] - LANE // 2
    base = packed_ref[:1, first : first + 2]
    reach_ref[...] = jnp.zeros_like(reach_ref)
    reach_ref[:rows, :hand_count] = own_ref[...]
    reach_ref[rows:, :hand_count] = mate_ref[...]
    row = lax.broadcasted_iota(jnp.int32, line_ref.shape, 0)
    within = jnp.where(row < rows, row, row - rows)
    line = jnp.where(row < rows, base[:, :1], base[:, 1:]) + within
    line_ref[...] = jnp.where(within < line_count, line, -2)


def first_kernel(hand_count, line_count, own_ref, mate_ref, *refs):
    tables, (packed_ref, own_out, mate_out, reach_ref, line_ref, same_ref), scratch = refs[:3], refs[3:9], refs[9:]
    same_ref[...] = packed_ref[...]
    lines_kernel(hand_count, line_count, own_ref, mate_ref, packed_ref, reach_ref, line_ref)
    add_boards(reach_ref, line_ref, *tables, packed_ref, None, own_out, mate_out, *scratch)


def more_kernel(reach_ref, line_ref, *refs):
    tables, (packed_ref, own_ref, mate_ref, own_out, mate_out), scratch = refs[:3], refs[3:8], refs[8:]
    add_boards(reach_ref, line_ref, *tables, packed_ref, (own_ref, mate_ref), own_out, mate_out, *scratch)


def add_boards(
    reach_ref, line_ref, apart_ref, collect_ref, spread_ref, packed_ref, earlier, own_out, mate_out, column_ref, board_ref
):
    wide, deep = apart_ref.shape[1], apart_ref.shape[0]
    rows = own_out.shape[0]
    parts = 1 + CARDS
    line = jnp.concatenate([line_ref[...]] * ((packed_ref.shape[1] - LANE - wide) // LANE), axis=1)
    lane = lax.broadcasted_iota(jnp.int32, (2 * rows, LANE), 1)
    board_total = packed_ref.shape[0]
    end = packed_ref.shape[1] - LANE
    slot = lax.broadcasted_iota(jnp.int32, (board_total, end - wide), 1)
    board_ref[:, :wide] = packed_ref[:, :wide]
    board_ref[:, wide:] = jnp.where(slot < packed_ref[:, wide - 1 : wide], packed_ref[:, wide:end], -1)

    zero, one = jnp.bfloat16(0), jnp.bfloat16(1)

    def order_keys(keys):
        ranks = keys & (RANK_SPAN - 1)
        live = (keys >> (RANK_SPAN.bit_length() - 1)).astype(jnp.float32)
        power = ranks >> (MANTISSA.bit_length() - 1)
        near = jnp.left_shift(1, jnp.minimum(power, 29)).astype(jnp.float32)
        far = jnp.left_shift(1, jnp.maximum(power - 29, 0)).astype(jnp.float32)
        return ((ranks & (MANTISSA - 1)) + MANTISSA).astype(jnp.float32) * near * far, live

    def add_board(column_ref, order, live, slots, before):
        order = order.astype(jnp.bfloat16)
        keep = jnp.max(jnp.where(slots == line, 1.0, 0.0), axis=1, keepdims=True)
        held = reach_ref[...] * live.astype(jnp.bfloat16) * keep.astype(jnp.bfloat16)
        show_reach = jnp.maximum(held, zero)
        fold_reach = jnp.maximum(-held, zero)
        sums = jnp.dot(fold_reach, collect_ref[...], preferred_element_type=jnp.float32)
        high = sums.astype(jnp.bfloat16).astype(jnp.float32)
        sums = jnp.where(lane < parts, high, sums - high).astype(jnp.bfloat16)
        for first, count in tiles(wide, COL_TILE):
            at = slice(first, first + count)
            total = 0.0
            for top, height in tiles(deep, ROW_TILE):
                down = slice(top, top + height)
                column = jnp.concatenate([column_ref[down]] * (count // LANE), axis=1)
                matrix = jnp.clip(order[:, at] - column, -one, one) * apart_ref[down, at]
                total += jnp.dot(show_reach[:, down], matrix, preferred_element_type=jnp.float32)
            total += jnp.dot(sums, spread_ref[:, at], preferred_element_type=jnp.float32)
            total = (total + fold_reach[:, at].astype(jnp.float32)) * live[:, at]
            if before is None:
                own_out[:, at] = total[:rows]
                mate_out[:, at] = total[rows:]
            else:
                own_out[:, at] = before[0][:, at] + total[:rows]
                mate_out[:, at] = before[1][:, at] + total[rows:]

    sums_here = (own_out, mate_out)
    if board_total <= UNROLL:
        orders, lives = order_keys(packed_ref[:, :wide])
        for board in range(board_total):
            row = slice(board, board + 1)
            turned = jnp.transpose(jnp.broadcast_to(orders[row], (LANE, wide)))
            column_ref[board] = turned[:deep].astype(jnp.bfloat16)
            slots = board_ref[row, wide:]
            add_board(column_ref.at[board], orders[row], lives[row], slots, sums_here if board else earlier)
    else:
        own_out[...] = jnp.zeros_like(own_out) if earlier is None else earlier[0][...]
        mate_out[...] = jnp.zeros_like(mate_out) if earlier is None else earlier[1][...]

        @pl.loop(0, board_total)
        def add_next(board):
            order, live = order_keys(board_ref[pl.ds(board, 1), :wide])
            column_ref[0] = jnp.transpose(jnp.broadcast_to(order, (LANE, wide)))[:deep].astype(jnp.bfloat16)
            add_board(column_ref.at[0], order, live, board_ref[pl.ds(board, 1), wide:], sums_here)


def board_sums(kernel, name, rows, inputs, tables, boards, sums=(), more=()):
    deep, wide = tables[0].shape
    out = [jax.ShapeDtypeStruct((rows, wide), jnp.float32)] * 2 + list(more)
    return pl.pallas_call(
        kernel,
        out_shape=out,
        in_specs=[WHOLE] * (len(inputs) + len(tables) + 1 + len(sums)),
        out_specs=[WHOLE] * len(out),
        scratch_shapes=[
            pltpu.VMEM((min(boards.shape[0], UNROLL), deep, LANE), jnp.bfloat16),
            pltpu.VMEM((boards.shape[0], boards.shape[1] - LANE), jnp.int32),
        ],
        compiler_params=params(32),
        name=name,
        cost_estimate=pl.CostEstimate(
            flops=4 * boards.shape[0] * rows * wide * wide, bytes_accessed=0, transcendentals=0
        ),
    )(*inputs, *tables, boards, *sums)


def powers():
    lane = lax.broadcasted_iota(jnp.int32, (1, LANE), 1)
    up_size, down_size = jnp.ones((1, LANE), jnp.float32), jnp.ones((1, LANE), jnp.float32)
    bit = 1
    while bit < LANE:
        chosen = (jnp.abs(lane - LOWEST) & bit) != 0
        up_size = jnp.where(chosen, up_size * 2.0**bit, up_size)
        down_size = jnp.where(chosen, down_size * 0.5**bit, down_size)
        bit *= 2
    return jnp.where(lane < LOWEST, down_size, up_size), jnp.where(lane < LOWEST, up_size, down_size)


def decide(hand_count, scale, own_ref, mate_ref, pot_ref, kind_ref, regret_ref):
    pot = as_column(pot_ref[...])
    coef = jnp.where(as_column(kind_ref[...]) == 1, -pot, pot) * scale
    values = (own_ref[:, :hand_count] + mate_ref[:, :hand_count]) * coef
    regrets = regret_ref[...]
    rows = regrets.shape[0]
    even = lax.broadcasted_iota(jnp.int32, (rows, 1), 0) % ACTS == 0

    def both(array):
        other = jnp.where(even, pltpu.roll(array, rows - 1, 0), pltpu.roll(array, 1, 0))
        return array + other

    positive = jnp.maximum(regrets, 0.0)
    strategy = (positive + floor_share) / (both(positive) + ACTS * floor_share)
    return regrets, values, both(strategy * values)


def regrets_kernel(hand_count, scale, *refs):
    regrets, values, node = decide(hand_count, scale, *refs[:-1])
    refs[-1][...] = jnp.maximum(regrets + values - node, 0.0)


def codes_kernel(hand_count, scale, *refs):
    *inputs, code_out, node_ref = refs
    _, _, node = decide(hand_count, scale, *inputs)
    rows = node.shape[0]
    size, flip = powers()
    largest = jnp.max(jnp.abs(node), axis=1, keepdims=True)
    place = jnp.sum(jnp.where(size < largest, 1.0, 0.0), axis=1, keepdims=True)
    lane = lax.broadcasted_iota(jnp.int32, (rows, LANE), 1).astype(jnp.float32)
    gain = jnp.sum(jnp.where(lane == place, flip, 0.0), axis=1, keepdims=True) * STEPS
    codes = node * gain
    for tile, (first, count) in enumerate(tiles(hand_count, LANE)):
        node_ref[tile, :, :count] = codes[:, first : first + count]
        if count < LANE:
            node_ref[tile, :, count:] = jnp.broadcast_to(place, (rows, LANE - count))
        picked = node_ref[tile, pl.ds(0, rows // ACTS, stride=ACTS), :]
        code_out[:, first : first + LANE] = jnp.floor(picked + 0.5).astype(jnp.int32).astype(jnp.int16)


def decision_call(kernel, name, hand_count, scale, out_shape, inputs, scratch=()):
    return pl.pallas_call(
        functools.partial(kernel, hand_count, scale),
        out_shape=out_shape,
        in_specs=[WHOLE] * len(inputs),
        out_specs=WHOLE,
        scratch_shapes=scratch,
        compiler_params=params(8),
        name=name,
    )(*inputs)


def chance_kernel(hand_count, order, *refs):
    code_refs, out_ref = refs[:-1], refs[-1]
    size, _ = powers()
    lane = lax.broadcasted_iota(jnp.int32, (out_ref.shape[0], LANE), 1)

    def value(ref):
        codes = ref[...].astype(jnp.int32)
        place = codes[:, hand_count : hand_count + 1]
        gain = jnp.sum(jnp.where(lane == place, size, 0.0), axis=1, keepdims=True)
        return codes[:, :hand_count].astype(jnp.float32) * (gain * (1.0 / (STEPS * len(code_refs))))

    values = {mask: value(ref) for mask, ref in zip((0, *order), code_refs)}
    total = None
    for mask in range(0, len(values), 2):
        pair = values[mask] + values[mask + 1]
        total = pair if total is None else total + pair
    out_ref[...] = total


def chance(hand_count, order, codes):
    return pl.pallas_call(
        functools.partial(chance_kernel, hand_count, order),
        out_shape=jax.ShapeDtypeStruct((codes[0].shape[0], hand_count), jnp.float32),
        in_specs=[WHOLE] * len(codes),
        out_specs=WHOLE,
        compiler_params=params(8),
        name="chance_sum",
    )(*codes)


def swap(array, axes, mask):
    return lax.ppermute(array, axes, [(index, index ^ mask) for index in range(lax.axis_size(axes))])


def on_device(
    regrets, opp_reach, pot_size, line_kind, board_lines, board_count, hand_ranks, live_hands
):
    hand_count = opp_reach.shape[2]
    line_count = opp_reach.shape[1]
    group = ("turn", "river")
    group_size = lax.axis_size(group)
    core = lax.axis_size("river")
    board_total = group_size * board_lines.shape[2]
    extra = up(line_count, SUB) - line_count
    bases = pass_on(first_lines(line_count, core))
    kinds = jnp.pad(line_kind, ((0, 0), (0, extra)))
    boards = pack(board_count[0, 0], board_lines[0, 0], hand_ranks[0, 0], live_hands[0, 0], bases)
    masks = [1 << bit for bit in range(group_size.bit_length() - 1) if 1 << bit != core]
    arrived = swap(boards, group, masks[0])
    reach, late_kinds, _ = lax.optimization_barrier((jnp.pad(opp_reach[0], ((0, extra), (0, 0))), kinds, bases))
    showdown = lax.broadcast_in_dim(late_kinds[0], reach.shape, (0,)) == 0
    reach = jnp.where(showdown, reach, -reach)
    pots = jnp.pad(pot_size, ((0, 0), (0, extra)))
    old_regrets = jnp.pad(regrets[0], ((0, extra), (0, 0)))
    mate_reach = swap(reach, group, core)
    held_tables = [jnp.asarray(table) for table in tables(hand_count)]
    rows, wide = reach.shape[0], up(hand_count, LANE)
    own, for_mate, all_reach, lines, boards = board_sums(
        functools.partial(first_kernel, hand_count, line_count),
        "first_boards",
        rows,
        (reach, mate_reach),
        held_tables,
        boards,
        more=(
            jax.ShapeDtypeStruct((2 * rows, wide), jnp.bfloat16),
            jax.ShapeDtypeStruct((2 * rows, LANE), jnp.int32),
            jax.ShapeDtypeStruct(boards.shape, boards.dtype),
        ),
    )
    for mask in (*masks[1:], None):
        latest = arrived
        if mask is not None:
            boards = jnp.concatenate([boards, latest], axis=0)
            arrived = swap(boards, group, mask)
        own, for_mate = board_sums(
            more_kernel, "more_boards", rows, (all_reach, lines), held_tables, latest, (own, for_mate)
        )
    mate = swap(for_mate, group, core)
    scale = 1.0 / (board_total * hand_count)
    inputs = (own, mate, pots, kinds, old_regrets)
    codes = decision_call(
        codes_kernel,
        "node_codes",
        hand_count,
        scale,
        jax.ShapeDtypeStruct((rows // ACTS, wide), jnp.int16),
        inputs,
        [pltpu.VMEM((wide // LANE, rows, LANE), jnp.float32)],
    )
    updated = decision_call(
        regrets_kernel, "new_regrets", hand_count, scale, jax.ShapeDtypeStruct((rows, hand_count), jnp.float32), inputs
    )
    order = (2, 3, 1)
    total = chance(hand_count, order, [codes] + [swap(codes, "flop", mask) for mask in order])
    return (updated[None, :line_count], total[: line_count // ACTS])


def solution(mesh):
    placed = (
        P("flop", ("turn", "river"), None),
        P("flop", ("turn", "river"), None),
        P("flop", ("turn", "river")),
        P("flop", ("turn", "river")),
        P("flop", "turn", "river", None),
        P("flop", "turn", "river"),
        P("flop", "turn", "river", None),
        P("flop", "turn", "river", None),
    )
    return jax.shard_map(
        on_device,
        mesh=mesh,
        in_specs=placed,
        out_specs=(P("flop", ("turn", "river"), None), P(("turn", "river"), None)),
        check_vma=False,
    )
```

```python
import functools

import jax
import jax.numpy as jnp
import numpy as np
from jax import lax
from jax.experimental import pallas as pl
from jax.experimental.pallas import tpu as pltpu
from jax.sharding import PartitionSpec as P

CARDS = 52
ACTS = 2
LANE = 128
SUB = 32
RANK_SPAN = 8192
MANTISSA = 128
ROW_TILE = 128
COL_TILE = 768
UNROLL = 8
STEPS = 32767.0
LOWEST = 100
WHOLE = pl.BlockSpec(memory_space=pltpu.VMEM)

floor_share = 0.1


def up(value, unit):
    return -(-value // unit) * unit


def tiles(total, size):
    return [(first, min(size, total - first)) for first in range(0, total, size)]


def params(mebibytes):
    return pltpu.CompilerParams(vmem_limit_bytes=mebibytes << 20)


@functools.cache
def tables(hand_count):
    wide, deep = up(hand_count, LANE), up(hand_count, 16)
    first, second = np.triu_indices(CARDS, 1)
    cards = np.zeros((hand_count, CARDS), np.float32)
    cards[np.arange(hand_count), first] = 1
    cards[np.arange(hand_count), second] = 1
    apart = np.zeros((deep, wide), np.float32)
    apart[:hand_count, :hand_count] = (cards @ cards.T) == 0
    spread = np.zeros((LANE, wide), np.float32)
    for first in (0, 1 + CARDS):
        spread[first, :hand_count] = 1
        spread[first + 1 : first + 1 + CARDS, :hand_count] = cards.T
    collect = -spread.T
    collect[:, [0, 1 + CARDS]] *= -1
    return [part.astype(jnp.bfloat16) for part in (apart, collect, spread)]


def as_column(row):
    size = row.shape[1]
    at = lax.broadcasted_iota(jnp.int32, (size, size), 0) == lax.broadcasted_iota(jnp.int32, (size, size), 1)
    return jnp.sum(jnp.where(at, row.astype(jnp.float32), 0.0), axis=1, keepdims=True)


def copy_all(pairs, sems):
    copies = [pltpu.make_async_copy(source, target, sems.at[at]) for at, (source, target) in enumerate(pairs)]
    for copy in copies:
        copy.start()
    for copy in copies:
        copy.wait()


def bases_kernel(line_count, core, out_ref):
    index = lax.axis_index("turn") * lax.axis_size("river") + lax.axis_index("river")
    lane = lax.broadcasted_iota(jnp.int32, out_ref.shape, 1)
    line = jnp.where(lane == LANE // 2, index, index ^ core) * line_count
    out_ref[...] = jnp.where((lane == LANE // 2) | (lane == LANE // 2 + 1), line, 0)


def first_lines(line_count, core):
    return pl.pallas_call(
        functools.partial(bases_kernel, line_count, core),
        out_shape=jax.ShapeDtypeStruct((1, LANE), jnp.int32),
        out_specs=WHOLE,
        compiler_params=params(4),
        name="first_lines",
        cost_estimate=pl.CostEstimate(flops=10 * 10**9, bytes_accessed=0, transcendentals=0),
    )()


def pass_kernel(in_ref, out_ref):
    out_ref[...] = in_ref[...]


def pass_on(array):
    return pl.pallas_call(
        pass_kernel,
        out_shape=jax.ShapeDtypeStruct(array.shape, array.dtype),
        in_specs=[WHOLE],
        out_specs=WHOLE,
        compiler_params=params(4),
        name="pass_on",
        cost_estimate=pl.CostEstimate(flops=60 * 10**9, bytes_accessed=0, transcendentals=0),
    )(array)


def pack(counts, slots, ranks, live, bases):
    hand_count, slot_count, boards = ranks.shape[1], slots.shape[1], ranks.shape[0]
    wide = up(hand_count, LANE)

    def place(array, first):
        after = wide + slot_count + LANE - first - array.shape[1]
        return jnp.pad(array, ((0, boards - array.shape[0]), (first, after)))

    packed = place(ranks, 0) + RANK_SPAN * place(live, 0) + place(slots, wide) + place(bases, wide + slot_count)
    lane = lax.broadcasted_iota(jnp.int32, packed.shape, 1)
    return jnp.where(lane == wide - 1, lax.broadcast_in_dim(counts, packed.shape, (0,)), packed)


def lines_kernel(hand_count, line_count, own_ref, mate_ref, packed_ref, reach_ref, line_ref):
    rows = own_ref.shape[0]
    first = packed_ref.shape[1] - LANE // 2
    base = packed_ref[:1, first : first + 2]
    reach_ref[...] = jnp.zeros_like(reach_ref)
    reach_ref[:rows, :hand_count] = own_ref[...]
    reach_ref[rows:, :hand_count] = mate_ref[...]
    row = lax.broadcasted_iota(jnp.int32, line_ref.shape, 0)
    within = jnp.where(row < rows, row, row - rows)
    line = jnp.where(row < rows, base[:, :1], base[:, 1:]) + within
    line_ref[...] = jnp.where(within < line_count, line, -2)


def first_kernel(hand_count, line_count, own_ref, mate_ref, *refs):
    tables, (packed_ref, own_out, mate_out, reach_ref, line_ref, same_ref), scratch = refs[:3], refs[3:9], refs[9:]
    same_ref[...] = packed_ref[...]
    lines_kernel(hand_count, line_count, own_ref, mate_ref, packed_ref, reach_ref, line_ref)
    add_boards(reach_ref, line_ref, *tables, packed_ref, None, own_out, mate_out, *scratch)


def more_kernel(reach_ref, line_ref, *refs):
    tables, (packed_ref, own_ref, mate_ref, own_out, mate_out), scratch = refs[:3], refs[3:8], refs[8:]
    add_boards(reach_ref, line_ref, *tables, packed_ref, (own_ref, mate_ref), own_out, mate_out, *scratch)


def add_boards(
    reach_ref, line_ref, apart_ref, collect_ref, spread_ref, packed_ref, earlier, own_out, mate_out, column_ref, board_ref
):
    wide, deep = apart_ref.shape[1], apart_ref.shape[0]
    rows = own_out.shape[0]
    parts = 1 + CARDS
    line = jnp.concatenate([line_ref[...]] * ((packed_ref.shape[1] - LANE - wide) // LANE), axis=1)
    lane = lax.broadcasted_iota(jnp.int32, (2 * rows, LANE), 1)
    board_total = packed_ref.shape[0]
    end = packed_ref.shape[1] - LANE
    slot = lax.broadcasted_iota(jnp.int32, (board_total, end - wide), 1)
    board_ref[:, :wide] = packed_ref[:, :wide]
    board_ref[:, wide:] = jnp.where(slot < packed_ref[:, wide - 1 : wide], packed_ref[:, wide:end], -1)

    zero, one = jnp.bfloat16(0), jnp.bfloat16(1)

    def order_keys(keys):
        ranks = keys & (RANK_SPAN - 1)
        live = (keys >> (RANK_SPAN.bit_length() - 1)).astype(jnp.float32)
        power = ranks >> (MANTISSA.bit_length() - 1)
        near = jnp.left_shift(1, jnp.minimum(power, 29)).astype(jnp.float32)
        far = jnp.left_shift(1, jnp.maximum(power - 29, 0)).astype(jnp.float32)
        return ((ranks & (MANTISSA - 1)) + MANTISSA).astype(jnp.float32) * near * far, live

    def add_board(column_ref, order, live, slots, before):
        order = order.astype(jnp.bfloat16)
        keep = jnp.max(jnp.where(slots == line, 1.0, 0.0), axis=1, keepdims=True)
        held = reach_ref[...] * live.astype(jnp.bfloat16) * keep.astype(jnp.bfloat16)
        show_reach = jnp.maximum(held, zero)
        fold_reach = jnp.maximum(-held, zero)
        sums = jnp.dot(fold_reach, collect_ref[...], preferred_element_type=jnp.float32)
        high = sums.astype(jnp.bfloat16).astype(jnp.float32)
        sums = jnp.where(lane < parts, high, sums - high).astype(jnp.bfloat16)
        for first, count in tiles(wide, COL_TILE):
            at = slice(first, first + count)
            total = 0.0
            for top, height in tiles(deep, ROW_TILE):
                down = slice(top, top + height)
                column = jnp.concatenate([column_ref[down]] * (count // LANE), axis=1)
                matrix = jnp.clip(order[:, at] - column, -one, one) * apart_ref[down, at]
                total += jnp.dot(show_reach[:, down], matrix, preferred_element_type=jnp.float32)
            total += jnp.dot(sums, spread_ref[:, at], preferred_element_type=jnp.float32)
            total = (total + fold_reach[:, at].astype(jnp.float32)) * live[:, at]
            if before is None:
                own_out[:, at] = total[:rows]
                mate_out[:, at] = total[rows:]
            else:
                own_out[:, at] = before[0][:, at] + total[:rows]
                mate_out[:, at] = before[1][:, at] + total[rows:]

    sums_here = (own_out, mate_out)
    if board_total <= UNROLL:
        orders, lives = order_keys(packed_ref[:, :wide])
        for board in range(board_total):
            row = slice(board, board + 1)
            turned = jnp.transpose(jnp.broadcast_to(orders[row], (LANE, wide)))
            column_ref[board] = turned[:deep].astype(jnp.bfloat16)
            slots = board_ref[row, wide:]
            add_board(column_ref.at[board], orders[row], lives[row], slots, sums_here if board else earlier)
    else:
        own_out[...] = jnp.zeros_like(own_out) if earlier is None else earlier[0][...]
        mate_out[...] = jnp.zeros_like(mate_out) if earlier is None else earlier[1][...]

        @pl.loop(0, board_total)
        def add_next(board):
            order, live = order_keys(board_ref[pl.ds(board, 1), :wide])
            column_ref[0] = jnp.transpose(jnp.broadcast_to(order, (LANE, wide)))[:deep].astype(jnp.bfloat16)
            add_board(column_ref.at[0], order, live, board_ref[pl.ds(board, 1), wide:], sums_here)


def board_sums(kernel, name, rows, inputs, tables, boards, sums=(), more=()):
    deep, wide = tables[0].shape
    out = [jax.ShapeDtypeStruct((rows, wide), jnp.float32)] * 2 + list(more)
    return pl.pallas_call(
        kernel,
        out_shape=out,
        in_specs=[WHOLE] * (len(inputs) + len(tables) + 1 + len(sums)),
        out_specs=[WHOLE] * len(out),
        scratch_shapes=[
            pltpu.VMEM((min(boards.shape[0], UNROLL), deep, LANE), jnp.bfloat16),
            pltpu.VMEM((boards.shape[0], boards.shape[1] - LANE), jnp.int32),
        ],
        compiler_params=params(32),
        name=name,
        cost_estimate=pl.CostEstimate(
            flops=4 * boards.shape[0] * rows * wide * wide, bytes_accessed=0, transcendentals=0
        ),
    )(*inputs, *tables, boards, *sums)


def powers():
    lane = lax.broadcasted_iota(jnp.int32, (1, LANE), 1)
    up_size, down_size = jnp.ones((1, LANE), jnp.float32), jnp.ones((1, LANE), jnp.float32)
    bit = 1
    while bit < LANE:
        chosen = (jnp.abs(lane - LOWEST) & bit) != 0
        up_size = jnp.where(chosen, up_size * 2.0**bit, up_size)
        down_size = jnp.where(chosen, down_size * 0.5**bit, down_size)
        bit *= 2
    return jnp.where(lane < LOWEST, down_size, up_size), jnp.where(lane < LOWEST, up_size, down_size)


def decide(hand_count, scale, own_ref, mate_ref, pot_ref, kind_ref, regret_ref):
    pot = as_column(pot_ref[...])
    coef = jnp.where(as_column(kind_ref[...]) == 1, -pot, pot) * scale
    values = (own_ref[:, :hand_count] + mate_ref[:, :hand_count]) * coef
    regrets = regret_ref[...]
    rows = regrets.shape[0]
    even = lax.broadcasted_iota(jnp.int32, (rows, 1), 0) % ACTS == 0

    def both(array):
        other = jnp.where(even, pltpu.roll(array, rows - 1, 0), pltpu.roll(array, 1, 0))
        return array + other

    positive = jnp.maximum(regrets, 0.0)
    strategy = (positive + floor_share) / (both(positive) + ACTS * floor_share)
    return regrets, values, both(strategy * values)


def regrets_kernel(hand_count, scale, *refs):
    regrets, values, node = decide(hand_count, scale, *refs[:-1])
    refs[-1][...] = jnp.maximum(regrets + values - node, 0.0)


def both(array):
    rows = array.shape[0]
    even = lax.broadcasted_iota(jnp.int32, (rows, 1), 0) % ACTS == 0
    return array + jnp.where(even, pltpu.roll(array, rows - 1, 0), pltpu.roll(array, 1, 0))


def weights_kernel(hand_count, scale, pot_ref, kind_ref, regret_ref, out_ref):
    pot = as_column(pot_ref[...])
    coef = jnp.where(as_column(kind_ref[...]) == 1, -pot, pot) * scale
    positive = jnp.maximum(regret_ref[...], 0.0)
    out_ref[...] = (positive + floor_share) * coef / (both(positive) + ACTS * floor_share)


def codes_kernel(hand_count, scale, own_ref, mate_ref, weight_ref, code_out, node_ref):
    node = both((own_ref[:, :hand_count] + mate_ref[:, :hand_count]) * weight_ref[...])
    rows = node.shape[0]
    size, flip = powers()
    largest = jnp.max(jnp.abs(node), axis=1, keepdims=True)
    place = jnp.sum(jnp.where(size < largest, 1.0, 0.0), axis=1, keepdims=True)
    lane = lax.broadcasted_iota(jnp.int32, (rows, LANE), 1).astype(jnp.float32)
    gain = jnp.sum(jnp.where(lane == place, flip, 0.0), axis=1, keepdims=True) * STEPS
    codes = node * gain
    for tile, (first, count) in enumerate(tiles(hand_count, LANE)):
        node_ref[tile, :, :count] = codes[:, first : first + count]
        if count < LANE:
            node_ref[tile, :, count:] = jnp.broadcast_to(place, (rows, LANE - count))
        picked = node_ref[tile, pl.ds(0, rows // ACTS, stride=ACTS), :]
        code_out[:, first : first + LANE] = jnp.floor(picked + 0.5).astype(jnp.int32).astype(jnp.int16)


def decision_call(kernel, name, hand_count, scale, out_shape, inputs, scratch=()):
    return pl.pallas_call(
        functools.partial(kernel, hand_count, scale),
        out_shape=out_shape,
        in_specs=[WHOLE] * len(inputs),
        out_specs=WHOLE,
        scratch_shapes=scratch,
        compiler_params=params(8),
        name=name,
    )(*inputs)


def chance_kernel(hand_count, order, *refs):
    code_refs, out_ref = refs[:-1], refs[-1]
    size, _ = powers()
    lane = lax.broadcasted_iota(jnp.int32, (out_ref.shape[0], LANE), 1)

    def value(ref):
        codes = ref[...].astype(jnp.int32)
        place = codes[:, hand_count : hand_count + 1]
        gain = jnp.sum(jnp.where(lane == place, size, 0.0), axis=1, keepdims=True)
        return codes[:, :hand_count].astype(jnp.float32) * (gain * (1.0 / (STEPS * len(code_refs))))

    values = {mask: value(ref) for mask, ref in zip((0, *order), code_refs)}
    total = None
    for mask in range(0, len(values), 2):
        pair = values[mask] + values[mask + 1]
        total = pair if total is None else total + pair
    out_ref[...] = total


def chance(hand_count, order, codes):
    return pl.pallas_call(
        functools.partial(chance_kernel, hand_count, order),
        out_shape=jax.ShapeDtypeStruct((codes[0].shape[0], hand_count), jnp.float32),
        in_specs=[WHOLE] * len(codes),
        out_specs=WHOLE,
        compiler_params=params(8),
        name="chance_sum",
    )(*codes)


def swap(array, axes, mask):
    return lax.ppermute(array, axes, [(index, index ^ mask) for index in range(lax.axis_size(axes))])


def on_device(
    regrets, opp_reach, pot_size, line_kind, board_lines, board_count, hand_ranks, live_hands
):
    hand_count = opp_reach.shape[2]
    line_count = opp_reach.shape[1]
    group = ("turn", "river")
    group_size = lax.axis_size(group)
    core = lax.axis_size("river")
    board_total = group_size * board_lines.shape[2]
    extra = up(line_count, SUB) - line_count
    bases = pass_on(first_lines(line_count, core))
    kinds = jnp.pad(line_kind, ((0, 0), (0, extra)))
    boards = pack(board_count[0, 0], board_lines[0, 0], hand_ranks[0, 0], live_hands[0, 0], bases)
    masks = [1 << bit for bit in range(group_size.bit_length() - 1) if 1 << bit != core]
    arrived = swap(boards, group, masks[0])
    reach, late_kinds, _ = lax.optimization_barrier((jnp.pad(opp_reach[0], ((0, extra), (0, 0))), kinds, bases))
    showdown = lax.broadcast_in_dim(late_kinds[0], reach.shape, (0,)) == 0
    reach = jnp.where(showdown, reach, -reach)
    pots = jnp.pad(pot_size, ((0, 0), (0, extra)))
    old_regrets = jnp.pad(regrets[0], ((0, extra), (0, 0)))
    mate_reach = swap(reach, group, core)
    held_tables = [jnp.asarray(table) for table in tables(hand_count)]
    rows, wide = reach.shape[0], up(hand_count, LANE)
    own, for_mate, all_reach, lines, boards = board_sums(
        functools.partial(first_kernel, hand_count, line_count),
        "first_boards",
        rows,
        (reach, mate_reach),
        held_tables,
        boards,
        more=(
            jax.ShapeDtypeStruct((2 * rows, wide), jnp.bfloat16),
            jax.ShapeDtypeStruct((2 * rows, LANE), jnp.int32),
            jax.ShapeDtypeStruct(boards.shape, boards.dtype),
        ),
    )
    scale = 1.0 / (board_total * hand_count)
    for mask in (*masks[1:], None):
        latest = arrived
        if mask is None:
            own, late_regrets, late_pots, late_kinds = lax.optimization_barrier((own, old_regrets, pots, kinds))
            weights = decision_call(
                weights_kernel,
                "line_weights",
                hand_count,
                scale,
                jax.ShapeDtypeStruct((rows, hand_count), jnp.float32),
                (late_pots, late_kinds, late_regrets),
            )
        if mask is not None:
            boards = jnp.concatenate([boards, latest], axis=0)
            arrived = swap(boards, group, mask)
        own, for_mate = board_sums(
            more_kernel, "more_boards", rows, (all_reach, lines), held_tables, latest, (own, for_mate)
        )
    mate = swap(for_mate, group, core)
    inputs = (own, mate, pots, kinds, old_regrets)
    codes = decision_call(
        codes_kernel,
        "node_codes",
        hand_count,
        scale,
        jax.ShapeDtypeStruct((rows // ACTS, wide), jnp.int16),
        (own, mate, weights),
        [pltpu.VMEM((wide // LANE, rows, LANE), jnp.float32)],
    )
    updated = decision_call(
        regrets_kernel, "new_regrets", hand_count, scale, jax.ShapeDtypeStruct((rows, hand_count), jnp.float32), inputs
    )
    order = (1, 3, 2)
    total = chance(hand_count, order, [codes] + [swap(codes, "flop", mask) for mask in order])
    return (updated[None, :line_count], total[: line_count // ACTS])


def solution(mesh):
    placed = (
        P("flop", ("turn", "river"), None),
        P("flop", ("turn", "river"), None),
        P("flop", ("turn", "river")),
        P("flop", ("turn", "river")),
        P("flop", "turn", "river", None),
        P("flop", "turn", "river"),
        P("flop", "turn", "river", None),
        P("flop", "turn", "river", None),
    )
    return jax.shard_map(
        on_device,
        mesh=mesh,
        in_specs=placed,
        out_specs=(P("flop", ("turn", "river"), None), P(("turn", "river"), None)),
        check_vma=False,
    )
```
